128 devices in a mesh: row: 8 (over z_hi, x), col: 16 (over y, z_lo, core).
Axes of the slice: x: 4, y: 4, z: 4 (z_hi: 2, z_lo: 2; z = z_hi * 2 + z_lo), core: 2. Of those that a mesh axis runs over, the one named last changes fastest.
Arguments:
- pixels_tokens: bfloat16 [4, 2304, 5120], P(None, 'col', 'row'), may hold values from -12 to 12, as said below
- ln_gain: float32 [5120], replicated, may hold values from 0.1 to 1.9
- ln_bias: float32 [5120], replicated, may hold values from -3 to 3
- w_qkv: bfloat16 [5120, 12288], P('col', 'row'), may hold values from -1 to 1, as said below
- w_out: bfloat16 [4096, 5120], P('col', 'row'), may hold values from -0.09375 to 0.09375
Outputs:
- block_out: bfloat16 [4, 2304, 5120], P(None, 'col', 'row')
The draws below stay inside these ranges and needn't reach their ends.
Inputs may be any that keep to these rules, and one draw needn't show every extreme that they name: `pixels_tokens`: activations of order one. `w_qkv`: projection entries scaled by the width.
All inputs are finite; a program needn't handle non-finite values.
Results may differ from the reference program's by a relative error of at most 0.012.
The reference program's roundings to bfloat16 on the way (of `normed`, `qkv`, `weights` and `heads_out`) count: a program that leaves them out, or rounds other values in their place, can miss the bound.
Values may be sent and summed in bfloat16 or wider, within the bound.
A program may use at most 128 MiB of HBM per device.

```python
import jax
import jax.numpy as jnp
from jax import lax

D = 5120
HDIM = 128
SEQ = 2304
IMAGES = 4
HEADS = 32


def draw_pixels_tokens(key, part):
    values = jax.random.normal(jax.random.fold_in(key, 1), (IMAGES, SEQ, D), jnp.float32)
    return jnp.clip(values, -12.0, 12.0).astype(jnp.bfloat16)


def draw_w_qkv(key, part):
    weights = jax.random.normal(jax.random.fold_in(key, 3), (D, HEADS * 3 * HDIM), jnp.float32) * (2.0 / jnp.sqrt(float(D)))
    return jnp.clip(weights, -1.0, 1.0).astype(jnp.bfloat16)


def shard_levels(own_key, extent, pieces, low, high):
    level, own = 1.0, jax.random.fold_in(own_key, 6)
    for position, parts in pieces:
        draws = jnp.exp(jax.random.uniform(jax.random.fold_in(own, position), (parts,), jnp.float32, low / len(pieces), high / len(pieces)))
        level = level * jnp.repeat(draws, extent[position] // parts).reshape([-1 if axis == position else 1 for axis in range(len(extent))])
    return level


def scatter_about(rng, dims, scale, limit, pieces=(), held_as=jnp.bfloat16):
    level = shard_levels(rng, dims, pieces, -0.22, 0.18) if pieces else 1.0
    drawn = jax.random.normal(rng, dims, jnp.float32) * scale * level
    return jnp.minimum(jnp.maximum(drawn, -limit), limit).astype(held_as)


def setup_inputs(seed: int = 0) -> dict:
    key_of = jax.random.split(jax.random.key(seed), 6)
    pixels_tokens = draw_pixels_tokens(jax.random.fold_in(key_of[5], 71), 0)
    ln_gain = jnp.clip(1.0 + 0.18 * jax.random.normal(key_of[1], (D,), jnp.float32), 0.1, 1.9)
    ln_bias = scatter_about(key_of[2], (D,), 0.5, 3.0, (), jnp.float32)
    w_qkv = draw_w_qkv(jax.random.fold_in(key_of[5], 71), 0)
    w_out = scatter_about(key_of[4], (HEADS * HDIM, D), (HEADS * HDIM) ** -0.5, 0.09375, ((0, 16), (1, 8)))
    return {"pixels_tokens": pixels_tokens, "ln_gain": ln_gain, "ln_bias": ln_bias, "w_qkv": w_qkv, "w_out": w_out}


def layer_norm(values, ln_gain, ln_bias):
    floats = values.astype(jnp.float32)
    center = lax.optimization_barrier(jnp.mean(floats, axis=-1, keepdims=True))
    spread = lax.optimization_barrier(jnp.mean((floats - center) * (floats - center), axis=-1, keepdims=True))
    return ((floats - center) * lax.rsqrt(spread + 1e-06) * ln_gain + ln_bias).astype(jnp.bfloat16)

def attend(triple):
    query, keys, values = (triple[0], triple[1], triple[2])
    scores = jnp.dot(query, keys.T, preferred_element_type=jnp.float32) * HDIM ** (-0.5)
    peak = lax.optimization_barrier(jnp.max(scores, axis=-1, keepdims=True))
    expo = jnp.exp(scores - peak)
    weights = (expo / lax.optimization_barrier(jnp.sum(expo, axis=-1, keepdims=True))).astype(jnp.bfloat16)
    return jnp.dot(weights, values, preferred_element_type=jnp.float32).astype(jnp.bfloat16)

def reference(pixels_tokens, ln_gain, ln_bias, w_qkv, w_out):
    normed = layer_norm(pixels_tokens, ln_gain, ln_bias).reshape(IMAGES * SEQ, D)
    qkv = jnp.dot(normed, w_qkv, preferred_element_type=jnp.float32).astype(jnp.bfloat16)
    qkv = qkv.reshape(IMAGES, SEQ, HEADS, 3, HDIM).transpose(0, 2, 3, 1, 4).reshape(IMAGES * HEADS, 3, SEQ, HDIM)
    heads_out = lax.map(attend, qkv)
    heads_out = heads_out.reshape(IMAGES, HEADS, SEQ, HDIM).transpose(0, 2, 1, 3).reshape(IMAGES * SEQ, HEADS * HDIM)
    projected = jnp.dot(heads_out, w_out, preferred_element_type=jnp.float32)
    summed = pixels_tokens.reshape(IMAGES * SEQ, D).astype(jnp.float32) + projected
    return summed.astype(jnp.bfloat16).reshape(IMAGES, SEQ, D)
```

```python
import jax
import jax.numpy as jnp
from jax import lax
from jax.experimental import pallas as pl
from jax.experimental.pallas import tpu as pltpu
from jax.sharding import PartitionSpec as P

HDIM = 128
MESH = pl.DeviceIdType.MESH
HALVES = (0, 1)
OWN, A, BP, BM, CP, CM, D, E = range(8)


def ring(p, step):
    return lax.rem(p + step + 4, 4)


class Gather:
    def __init__(self, p, q, device, block, view, source, sems, last_by_pair, sibling=None):
        self.p, self.q, self.device, self.block = p, q, device, block
        self.view, self.source, self.sems = view, source, sems
        self.last_by_pair, self.sibling = last_by_pair, sibling
        self.sent = []

    def place(self, role):
        p, q, o = self.p, self.q, 1 - self.q
        return {
            OWN: (p, q), A: (p, o), BP: (ring(p, -1), q), BM: (ring(p, 1), q),
            CP: (ring(p, -1), o), CM: (ring(p, 1), o), D: (ring(p, 2), q), E: (ring(p, 2), o),
        }[role]

    def ref(self, role, half):
        return self.view(self.block(*self.place(role)), half)

    def send(self, role, half, there, to):
        send_sem, recv_sem = self.sems[0], self.sems[1]
        src = self.source(half) if role == OWN and self.source is not None else self.ref(role, half)
        copy = pltpu.make_async_remote_copy(
            src_ref=src,
            dst_ref=self.ref(role, half),
            send_sem=send_sem.at[there, half],
            recv_sem=recv_sem.at[there, half],
            device_id=to,
            device_id_type=MESH,
        )
        copy.start()
        self.sent.append(copy)

    def share(self, role, half):
        if self.sibling is None:
            return
        device, view = self.sibling
        send_sem, recv_sem = self.sems[2], self.sems[3]
        src = self.source(half) if role == OWN and self.source is not None else self.ref(role, half)
        copy = pltpu.make_async_remote_copy(
            src_ref=src,
            dst_ref=self.ref(role, half),
            send_sem=send_sem.at[role, half],
            recv_sem=recv_sem.at[role, half],
            device_id=device,
            device_id_type=MESH,
        )
        copy.start()
        self.sent.append(copy)

    def up(self):
        return self.device(ring(self.p, 1), self.q)

    def down(self):
        return self.device(ring(self.p, -1), self.q)

    def across(self):
        return self.device(self.p, 1 - self.q)

    def begin(self, half):
        self.send(OWN, half, A, self.across())
        self.send(OWN, half, BP, self.up())
        self.send(OWN, half, BM, self.down())
        self.share(OWN, half)

    def arrive(self, role, half):
        recv_sem = self.sems[1]
        here = self.ref(role, half)
        pltpu.make_async_copy(here, here, recv_sem.at[role, half]).wait()
        if role == A:
            self.send(A, half, CP, self.up())
            self.send(A, half, CM, self.down())
        elif role == BP and half == 0:
            self.send(BP, half, D, self.up())
        elif role == BM and half == 1:
            self.send(BM, half, D, self.down())
        elif role == D and self.last_by_pair:
            self.send(D, half, E, self.across())
        elif role == CP and half == 0 and not self.last_by_pair:
            self.send(CP, half, E, self.up())
        elif role == CM and half == 1 and not self.last_by_pair:
            self.send(CM, half, E, self.down())
        self.share(role, half)

    def shared(self, role):
        _, view = self.sibling
        for half in HALVES:
            here = view(self.place(role), half)
            pltpu.make_async_copy(here, here, self.sems[3].at[role, half]).wait()

    def finish(self):
        for copy in self.sent:
            copy.wait_send()


def block_kernel(
    x_ref, gain_ref, bias_ref, wq_ref, wo_ref, out_ref,
    xbuf, nbuf, wbuf, wobuf, acc, qkv, item, hout, hbuf, pacc,
    xs, xr, ws, wr, wss, wsr, os, orr, oss, osr, hs, hr,
    as_, ar, bs, br, local_sem,
):
    row, col = lax.axis_index("row"), lax.axis_index("col")
    zh, xx = lax.div(row, 4), lax.rem(row, 4)
    yy, zl, core = lax.div(col, 4), lax.rem(lax.div(col, 2), 2), lax.rem(col, 2)
    tokens, feat = x_ref.shape
    wrows, wcols = wq_ref.shape
    orows, ocols = wo_ref.shape
    seq_col = tokens // 4
    per_head = 3 * HDIM

    def col_device(y, z):
        return (row, y * 4 + z * 2 + core)

    def row_device(x, h):
        return (h * 4 + x, col)

    def col_peer(d):
        return lax.rem(col + d, 16)

    barrier = pltpu.get_barrier_semaphore()
    for d in range(1, 16):
        pl.semaphore_signal(barrier, inc=1, device_id=(row, col_peer(d)), device_id_type=MESH)
    for peer in (row_device(ring(xx, 1), zh), row_device(ring(xx, -1), zh), row_device(xx, 1 - zh)):
        pl.semaphore_signal(barrier, inc=1, device_id=peer, device_id_type=MESH)

    def cols(ref, start, size, rows=None):
        rows = pl.ds(0, tokens) if rows is None else rows
        return ref.at[rows, pl.ds(pl.multiple_of(start, 128), size)]

    def weight_view(buf, rows, k):
        half_rows = rows // 2

        def view(place, half):
            start = (place[0] * 4 + place[1] * 2 + k) * rows + half * half_rows
            return buf.at[pl.ds(pl.multiple_of(start, 16), half_rows)]

        return view

    def weight_gather(src, buf, sems, last_by_pair):
        rows = src.shape[0]
        return Gather(
            yy, zl, col_device, lambda y, z: (y, z), weight_view(buf, rows, core),
            lambda half: src.at[pl.ds(half * (rows // 2), rows // 2)], sems, last_by_pair,
            sibling=((row, yy * 4 + zl * 2 + 1 - core), weight_view(buf, rows, 1 - core)),
        )

    half_tokens = tokens // 2

    def row_gather(buf, width, source, sems, last_by_pair):
        return Gather(
            xx, zh, row_device, lambda x, h: h * 4 + x,
            lambda b, half: cols(buf, b * width, width, pl.ds(half * half_tokens, half_tokens)),
            source, sems, last_by_pair,
        )

    gx = row_gather(xbuf, feat, lambda half: x_ref.at[pl.ds(half * half_tokens, half_tokens)], (xs, xr), False)
    gw = weight_gather(wq_ref, wbuf, (ws, wr, wss, wsr), True)
    go = weight_gather(wo_ref, wobuf, (os, orr, oss, osr), False)
    gh = row_gather(hbuf, 4 * HDIM, None, (hs, hr), True)

    own = [
        pltpu.make_async_copy(x_ref, cols(xbuf, row * feat, feat), local_sem.at[0]),
        pltpu.make_async_copy(wq_ref, wbuf.at[pl.ds(pl.multiple_of(col * wrows, 16), wrows)], local_sem.at[1]),
        pltpu.make_async_copy(wo_ref, wobuf.at[pl.ds(pl.multiple_of(col * orows, 16), orows)], local_sem.at[2]),
    ]
    for copy in own:
        copy.start()
    pl.semaphore_wait(barrier, 18)

    for half in HALVES:
        gx.begin(half)
        gw.begin(half)
    for copy in own:
        copy.wait()
    for half in HALVES:
        for role in (BP, BM, A):
            gx.arrive(role, half)
        for role in (BP, BM):
            gw.arrive(role, half)
        gw.arrive(A, half)
    gw.arrive(D, 0)
    gw.arrive(D, 1)
    for half in HALVES:
        gx.arrive(CP, half)
        gx.arrive(CM, half)
    for role in (D, E):
        for half in HALVES:
            gx.arrive(role, half)

    width = xbuf.shape[1]

    @pl.loop(0, tokens // 16)
    def _(i):
        rows = pl.ds(pl.multiple_of(i * 16, 16), 16)
        floats = xbuf[rows, :].astype(jnp.float32)
        center = jnp.sum(floats, axis=-1, keepdims=True) * (1.0 / width)
        moved = floats - center
        spread = jnp.sum(moved * moved, axis=-1, keepdims=True) * (1.0 / width)
        nbuf[rows, :] = (moved * lax.rsqrt(spread + 1e-06) * gain_ref[...] + bias_ref[...]).astype(jnp.bfloat16)

    unit = 2 * wrows

    def product(place, columns):
        at = pl.multiple_of((place[0] * 2 + place[1]) * unit, 128)
        return jnp.dot(
            nbuf[:, pl.ds(at, unit)], wbuf[pl.ds(at, unit), columns], preferred_element_type=jnp.float32
        )

    def multiply(role, first=False):
        gw.shared(role)
        place = gw.place(role)

        @pl.loop(0, wcols // per_head)
        def _(j):
            columns = pl.ds(pl.multiple_of(j * per_head, 128), per_head)
            if first:
                acc[:, columns] = product(place, columns)
            else:
                acc[:, columns] += product(place, columns)

    multiply(OWN, first=True)
    multiply(A)
    multiply(BP)
    multiply(BM)
    gw.arrive(CP, 0)
    gw.arrive(CM, 0)
    multiply(D)
    gw.arrive(E, 0)
    gw.arrive(E, 1)
    gw.arrive(CP, 1)
    gw.arrive(CM, 1)
    multiply(E)
    multiply(CP)
    gw.shared(CM)

    def item_rows(c):
        return pl.ds(pl.multiple_of(c * seq_col, 16), seq_col)

    head = lax.rem(col, 4)
    for j in range(4):
        columns = pl.ds(j * per_head, per_head)
        qkv[:, columns] = (acc[:, columns] + product(gw.place(CM), columns)).astype(jnp.bfloat16)

    def to_attend(d):
        c = col_peer(d)
        src = qkv.at[item_rows(lax.div(c, 4)), pl.ds(pl.multiple_of(lax.rem(c, 4) * per_head, 128), per_head)]
        return src, (row, c)

    attending = []
    for d in range(1, 16):
        src, device = to_attend(d)
        copy = pltpu.make_async_remote_copy(
            src_ref=src, dst_ref=item.at[item_rows(col)], send_sem=as_.at[d], recv_sem=ar.at[d],
            device_id=device, device_id_type=MESH,
        )
        copy.start()
        attending.append(copy)
    src, _ = to_attend(0)
    mine = pltpu.make_async_copy(src, item.at[item_rows(col)], local_sem.at[0])
    mine.start()
    mine.wait()
    for d in range(1, 16):
        here = item.at[item_rows(lax.rem(col - d + 16, 16))]
        pltpu.make_async_copy(here, here, ar.at[d]).wait()

    for half in HALVES:
        go.begin(half)

    def back_view(c):
        return hbuf.at[item_rows(lax.div(c, 4)), pl.ds(pl.multiple_of((row * 4 + lax.rem(c, 4)) * HDIM, 128), HDIM)]

    def back(d):
        c = col_peer(d)
        return pltpu.make_async_remote_copy(
            src_ref=hout.at[item_rows(c)], dst_ref=back_view(col), send_sem=bs.at[d], recv_sem=br.at[d],
            device_id=(row, c), device_id_type=MESH,
        )

    scale = HDIM ** (-0.5)

    def attend(c):
        rows = item_rows(c)
        scores = lax.dot_general(
            item[rows, :HDIM], item[:, HDIM : 2 * HDIM], (((1,), (1,)), ((), ())),
            preferred_element_type=jnp.float32,
        )
        peak = jnp.max(scores, axis=-1, keepdims=True)
        expo = jnp.exp((scores - peak) * scale)
        total = jnp.sum(expo, axis=-1, keepdims=True)
        mixed = jnp.dot(expo.astype(jnp.bfloat16), item[:, 2 * HDIM :], preferred_element_type=jnp.float32)
        hout[rows, :] = (mixed / total).astype(jnp.bfloat16)

    @pl.loop(1, 16)
    def _(d):
        attend(col_peer(d))
        back(d).start()

    attend(col)
    mine = pltpu.make_async_copy(hout.at[item_rows(col)], back_view(col), local_sem.at[0])
    mine.start()
    for half in HALVES:
        for role in (BP, BM, A):
            go.arrive(role, half)
    mine.wait()
    for d in range(1, 16):
        here = back_view(lax.rem(col - d + 16, 16))
        pltpu.make_async_copy(here, here, br.at[d]).wait()

    for half in HALVES:
        gh.begin(half)
    for half in HALVES:
        for role in (CP, CM):
            go.arrive(role, half)
    for role in (D, E):
        for half in HALVES:
            go.arrive(role, half)
    for role in range(8):
        go.shared(role)

    def project(role, first=False):
        at = pl.multiple_of(gh.block(*gh.place(role)) * 4 * HDIM, 128)
        part = jnp.dot(
            hbuf[:, pl.ds(at, 4 * HDIM)], wobuf[pl.ds(at, 4 * HDIM), :], preferred_element_type=jnp.float32
        )
        if first:
            pacc[...] = part
        else:
            pacc[...] += part

    project(OWN, first=True)
    for half in HALVES:
        for role in (BP, BM, A):
            gh.arrive(role, half)
    for role in (BP, BM, A):
        project(role)
    gh.arrive(D, 0)
    gh.arrive(D, 1)
    project(D)
    for half in HALVES:
        gh.arrive(CP, half)
        gh.arrive(CM, half)
    project(CP)
    project(CM)
    gh.arrive(E, 0)
    gh.arrive(E, 1)
    at = pl.multiple_of(gh.block(*gh.place(E)) * 4 * HDIM, 128)
    part = jnp.dot(hbuf[:, pl.ds(at, 4 * HDIM)], wobuf[pl.ds(at, 4 * HDIM), :], preferred_element_type=jnp.float32)
    residual = xbuf[:, pl.ds(pl.multiple_of(row * feat, 128), feat)].astype(jnp.float32)
    out_ref[...] = (residual + (pacc[...] + part)).astype(jnp.bfloat16)

    for gather in (gx, gw, go, gh):
        gather.finish()
    for copy in attending:
        copy.wait_send()
    for d in range(1, 16):
        back(d).wait_send()


def local(pixels_tokens, ln_gain, ln_bias, w_qkv, w_out):
    images, seq_col, feat = pixels_tokens.shape
    tokens = images * seq_col
    rows, cols = lax.axis_size("row"), lax.axis_size("col")
    bf16, f32 = jnp.bfloat16, jnp.float32
    width = rows * feat
    wcols, ocols = w_qkv.shape[1], w_out.shape[1]
    heads = cols * w_out.shape[0]
    dma = pltpu.SemaphoreType.DMA
    any_space = pl.BlockSpec(memory_space=pl.ANY)
    vmem = pl.BlockSpec(memory_space=pltpu.VMEM)
    pairs = [dma((8, 2)), dma((8, 2))]
    out = pl.pallas_call(
        block_kernel,
        out_shape=jax.ShapeDtypeStruct((tokens, feat), bf16),
        in_specs=[any_space, vmem, vmem, any_space, any_space],
        out_specs=vmem,
        scratch_shapes=[
            pltpu.VMEM((tokens, width), bf16),
            pltpu.VMEM((tokens, width), bf16),
            pltpu.VMEM((width, wcols), bf16),
            pltpu.VMEM((heads, ocols), bf16),
            pltpu.VMEM((tokens, wcols), f32),
            pltpu.VMEM((tokens, wcols), bf16),
            pltpu.VMEM((cols * seq_col, 3 * HDIM), bf16),
            pltpu.VMEM((cols * seq_col, HDIM), bf16),
            pltpu.VMEM((tokens, heads), bf16),
            pltpu.VMEM((tokens, ocols), f32),
            *pairs, *pairs, *pairs, *pairs, *pairs, *pairs,
            dma((16,)), dma((16,)), dma((16,)), dma((16,)), dma((3,)),
        ],
        compiler_params=pltpu.CompilerParams(
            collective_id=0, has_side_effects=True, vmem_limit_bytes=60 * 2**20
        ),
        name="attention_block",
    )(pixels_tokens.reshape(tokens, feat), ln_gain.reshape(1, -1), ln_bias.reshape(1, -1), w_qkv, w_out)
    return out.reshape(images, seq_col, feat)


def solution(mesh):
    in_specs = (P(None, "col", "row"), P(), P(), P("col", "row"), P("col", "row"))
    out_specs = P(None, "col", "row")
    return jax.shard_map(local, mesh=mesh, in_specs=in_specs, out_specs=out_specs, check_vma=False)
```

```python
import jax
import jax.numpy as jnp
from jax import lax
from jax.experimental import pallas as pl
from jax.experimental.pallas import tpu as pltpu
from jax.sharding import PartitionSpec as P

HDIM = 128
MESH = pl.DeviceIdType.MESH
HALVES = (0, 1)
OWN, A, BP, BM, CP, CM, D, E = range(8)


def ring(p, step):
    return lax.rem(p + step + 4, 4)


class Gather:
    def __init__(self, p, q, device, block, view, source, sems, last_by_pair, sibling=None):
        self.p, self.q, self.device, self.block = p, q, device, block
        self.view, self.source, self.sems = view, source, sems
        self.last_by_pair, self.sibling = last_by_pair, sibling
        self.sent = []

    def place(self, role):
        p, q, o = self.p, self.q, 1 - self.q
        return {
            OWN: (p, q), A: (p, o), BP: (ring(p, -1), q), BM: (ring(p, 1), q),
            CP: (ring(p, -1), o), CM: (ring(p, 1), o), D: (ring(p, 2), q), E: (ring(p, 2), o),
        }[role]

    def ref(self, role, half):
        return self.view(self.block(*self.place(role)), half)

    def send(self, role, half, there, to):
        send_sem, recv_sem = self.sems[0], self.sems[1]
        src = self.source(half) if role == OWN and self.source is not None else self.ref(role, half)
        copy = pltpu.make_async_remote_copy(
            src_ref=src,
            dst_ref=self.ref(role, half),
            send_sem=send_sem.at[there, half],
            recv_sem=recv_sem.at[there, half],
            device_id=to,
            device_id_type=MESH,
        )
        copy.start()
        self.sent.append(copy)

    def share(self, role, half):
        if self.sibling is None:
            return
        device, view = self.sibling
        send_sem, recv_sem = self.sems[2], self.sems[3]
        src = self.source(half) if role == OWN and self.source is not None else self.ref(role, half)
        copy = pltpu.make_async_remote_copy(
            src_ref=src,
            dst_ref=self.ref(role, half),
            send_sem=send_sem.at[role, half],
            recv_sem=recv_sem.at[role, half],
            device_id=device,
            device_id_type=MESH,
        )
        copy.start()
        self.sent.append(copy)

    def up(self):
        return self.device(ring(self.p, 1), self.q)

    def down(self):
        return self.device(ring(self.p, -1), self.q)

    def across(self):
        return self.device(self.p, 1 - self.q)

    def begin(self, half):
        self.send(OWN, half, A, self.across())
        self.send(OWN, half, BP, self.up())
        self.send(OWN, half, BM, self.down())
        self.share(OWN, half)

    def arrive(self, role, half):
        recv_sem = self.sems[1]
        here = self.ref(role, half)
        pltpu.make_async_copy(here, here, recv_sem.at[role, half]).wait()
        if role == A:
            self.send(A, half, CP, self.up())
            self.send(A, half, CM, self.down())
        elif role == BP and half == 0:
            self.send(BP, half, D, self.up())
        elif role == BM and half == 1:
            self.send(BM, half, D, self.down())
        elif role == D and self.last_by_pair:
            self.send(D, half, E, self.across())
        elif role == CP and half == 0 and not self.last_by_pair:
            self.send(CP, half, E, self.up())
        elif role == CM and half == 1 and not self.last_by_pair:
            self.send(CM, half, E, self.down())
        self.share(role, half)

    def shared(self, role):
        _, view = self.sibling
        for half in HALVES:
            here = view(self.place(role), half)
            pltpu.make_async_copy(here, here, self.sems[3].at[role, half]).wait()

    def finish(self):
        for copy in self.sent:
            copy.wait_send()


def block_kernel(
    x_ref, gain_ref, bias_ref, wq_ref, wo_ref, out_ref,
    xbuf, nbuf, wbuf, wobuf, acc, qkv, item0, item1, hout0, hout1, heads0, heads1, pacc,
    stats, moments,
    xs, xr, ws, wr, wss, wsr, os, orr, oss, osr, hs0, hr0, hs1, hr1,
    as_, ar, ass, asr, bs, br, ms, mr, local_sem,
):
    row, col = lax.axis_index("row"), lax.axis_index("col")
    zh, xx = lax.div(row, 4), lax.rem(row, 4)
    yy, zl, core = lax.div(col, 4), lax.rem(lax.div(col, 2), 2), lax.rem(col, 2)
    plane = lax.div(col, 2)
    tokens, feat = x_ref.shape
    wrows, wcols = wq_ref.shape
    orows, ocols = wo_ref.shape
    seq_col = tokens // 4
    per_head = 3 * HDIM
    items, houts, heads = (item0, item1), (hout0, hout1), (heads0, heads1)
    sibling = (row, plane * 2 + 1 - core)

    def col_device(y, z):
        return (row, y * 4 + z * 2 + core)

    def row_device(x, h):
        return (h * 4 + x, col)

    def plane_peer(d):
        return lax.rem(plane + d, 8)

    def plane_device(p):
        return (row, p * 2 + core)

    def row_peer(d):
        return (lax.rem(row + d, 8), col)

    barrier = pltpu.get_barrier_semaphore()
    for d in range(1, 8):
        pl.semaphore_signal(barrier, inc=1, device_id=plane_device(plane_peer(d)), device_id_type=MESH)
        pl.semaphore_signal(barrier, inc=1, device_id=row_peer(d), device_id_type=MESH)
    pl.semaphore_signal(barrier, inc=1, device_id=sibling, device_id_type=MESH)

    def cols(ref, start, size, rows=None):
        rows = pl.ds(0, tokens) if rows is None else rows
        return ref.at[rows, pl.ds(pl.multiple_of(start, 128), size)]

    half_rows = wrows // 2

    def wq_view(k):
        def view(place, half):
            start = (place[0] * 4 + place[1] * 2 + k) * wrows + half * half_rows
            return wbuf.at[pl.ds(pl.multiple_of(start, 16), half_rows)]

        return view

    def wo_view(k):
        def view(place, half):
            start = (place[0] * 4 + place[1] * 2 + k) * HDIM
            return wobuf.at[half, pl.ds(pl.multiple_of(start, 16), HDIM)]

        return view

    def weight_gather(src, view, sems, last_by_pair):
        size = src.shape[0] // 2
        return Gather(
            yy, zl, col_device, lambda y, z: (y, z), view(core),
            lambda half: src.at[pl.ds(half * size, size)], sems, last_by_pair,
            sibling=(sibling, view(1 - core)),
        )

    half_tokens = tokens // 2

    def row_gather(buf, width, source, sems, last_by_pair):
        return Gather(
            xx, zh, row_device, lambda x, h: h * 4 + x,
            lambda b, half: cols(buf, b * width, width, pl.ds(half * half_tokens, half_tokens)),
            source, sems, last_by_pair,
        )

    gx = row_gather(xbuf, feat, lambda half: x_ref.at[pl.ds(half * half_tokens, half_tokens)], (xs, xr), False)
    gw = weight_gather(wq_ref, wq_view, (ws, wr, wss, wsr), True)
    go = weight_gather(wo_ref, wo_view, (os, orr, oss, osr), False)
    gh = [
        row_gather(heads0, 2 * HDIM, None, (hs0, hr0), True),
        row_gather(heads1, 2 * HDIM, None, (hs1, hr1), True),
    ]

    own = [
        pltpu.make_async_copy(x_ref, cols(xbuf, row * feat, feat), local_sem.at[0]),
        pltpu.make_async_copy(wq_ref, wbuf.at[pl.ds(pl.multiple_of(col * wrows, 16), wrows)], local_sem.at[1]),
        pltpu.make_async_copy(wo_ref.at[pl.ds(0, HDIM)], wo_view(core)((yy, zl), 0), local_sem.at[2]),
        pltpu.make_async_copy(wo_ref.at[pl.ds(HDIM, HDIM)], wo_view(core)((yy, zl), 1), local_sem.at[3]),
    ]
    for copy in own:
        copy.start()
    pl.semaphore_wait(barrier, 15)

    for half in HALVES:
        gx.begin(half)
        gw.begin(half)
    for copy in own:
        copy.wait()

    padded = moments.shape[0]
    moments[...] = jnp.zeros_like(moments)

    @pl.loop(0, tokens // 32)
    def _(i):
        rows = pl.ds(pl.multiple_of(i * 32, 32), 32)
        floats = xbuf[rows, pl.ds(pl.multiple_of(row * feat, 128), feat)].astype(jnp.float32)
        center = jnp.sum(floats, axis=-1, keepdims=True) * (1.0 / feat)
        moved = floats - center
        square = jnp.sum(moved * moved, axis=-1, keepdims=True)
        lane = lax.broadcasted_iota(jnp.int32, (32, 128), 1)
        moments[rows, :] = jnp.where(lane == 0, center, jnp.where(lane == 1, square, 0.0))

    stats[row] = moments[...].T[:8]
    told = []
    for d in range(1, 8):
        copy = pltpu.make_async_remote_copy(
            src_ref=stats.at[row], dst_ref=stats.at[row], send_sem=ms.at[d], recv_sem=mr.at[d],
            device_id=row_peer(d), device_id_type=MESH,
        )
        copy.start()
        told.append(copy)
    for item in items:
        item[:, 3 * HDIM :] = jnp.ones((item.shape[0], HDIM), jnp.bfloat16)

    for role in (BP, BM, A):
        gx.arrive(role, 0)
    for role in (BP, BM, A):
        gw.arrive(role, 0)
    for d in range(1, 8):
        here = stats.at[lax.rem(row - d + 8, 8)]
        pltpu.make_async_copy(here, here, mr.at[d]).wait()
    centers = stats[:, 0, :]
    mean = jnp.sum(centers, axis=0, keepdims=True) * (1.0 / 8)
    off = centers - mean
    square = jnp.sum(stats[:, 1, :], axis=0, keepdims=True) + jnp.sum(off * off, axis=0, keepdims=True) * feat
    rate = lax.rsqrt(square * (1.0 / (8 * feat)) + 1e-06)
    line = lax.broadcasted_iota(jnp.int32, (128, padded), 0)
    moments[...] = jnp.where(line == 0, mean, rate).T

    def normalise(role):
        columns = pl.ds(pl.multiple_of(gx.block(*gx.place(role)) * feat, 128), feat)
        gain, bias = gain_ref[:, columns], bias_ref[:, columns]

        @pl.loop(0, tokens // 32)
        def _(i):
            rows = pl.ds(pl.multiple_of(i * 32, 32), 32)
            floats = xbuf[rows, columns].astype(jnp.float32)
            nbuf[rows, columns] = (
                (floats - moments[rows, 0:1]) * moments[rows, 1:2] * gain + bias
            ).astype(jnp.bfloat16)

    normalise(OWN)
    for role in (BP, BM, A):
        gx.arrive(role, 1)
    for role in (BP, BM, A):
        gw.arrive(role, 1)
    gw.arrive(D, 0)
    gw.arrive(D, 1)
    normalise(BP)
    normalise(BM)
    for half in HALVES:
        gx.arrive(CP, half)
        gx.arrive(CM, half)
    normalise(A)
    for half in HALVES:
        gx.arrive(D, half)
    for role in (CP, CM, D):
        normalise(role)
    for half in HALVES:
        gx.arrive(E, half)
    normalise(E)

    unit = 2 * wrows

    def product(place, columns):
        at = pl.multiple_of((place[0] * 2 + place[1]) * unit, 128)
        return jnp.dot(
            nbuf[:, pl.ds(at, unit)], wbuf[pl.ds(at, unit), columns], preferred_element_type=jnp.float32
        )

    def multiply(role, first=False):
        gw.shared(role)
        place = gw.place(role)

        @pl.loop(0, wcols // per_head)
        def _(j):
            columns = pl.ds(pl.multiple_of(j * per_head, 128), per_head)
            if first:
                acc[:, columns] = product(place, columns)
            else:
                acc[:, columns] += product(place, columns)

    multiply(OWN, first=True)
    multiply(BP)
    multiply(BM)
    multiply(A)
    gw.arrive(CP, 0)
    gw.arrive(CM, 0)
    multiply(D)
    gw.arrive(E, 0)
    gw.arrive(CP, 1)
    gw.arrive(CM, 1)
    gw.arrive(E, 1)
    for role in (CP, CM, E):
        gw.shared(role)

    def rows_of(p):
        return pl.ds(pl.multiple_of(p * seq_col, 16), seq_col)

    def to_attend(wave, d):
        p = plane_peer(d)
        start = pl.multiple_of((lax.rem(p, 2) * 2 + wave) * per_head, 128)
        src = qkv.at[rows_of(lax.div(p, 2)), pl.ds(start, per_head)]
        dst = items[wave].at[rows_of(plane), pl.ds(0, per_head)]
        return src, dst, plane_device(p)

    attending = []

    def attend_send(wave):
        for z in range(2):
            columns = pl.ds((z * 2 + wave) * per_head, per_head)
            total = acc[:, columns]
            for role in (CP, CM, E):
                total += product(gw.place(role), columns)
            qkv[:, columns] = total.astype(jnp.bfloat16)
        src, dst, _ = to_attend(wave, 0)
        mine = pltpu.make_async_copy(src, dst, local_sem.at[wave])
        mine.start()
        for d in range(1, 8):
            src, dst, device = to_attend(wave, d)
            copy = pltpu.make_async_remote_copy(
                src_ref=src, dst_ref=dst, send_sem=as_.at[wave, d], recv_sem=ar.at[wave, d],
                device_id=device, device_id_type=MESH,
            )
            copy.start()
            attending.append(copy)
        return mine

    both = pl.ds(HDIM, 2 * HDIM)

    def keys_share(wave, d):
        p = lax.rem(plane - d + 8, 8)
        copy = pltpu.make_async_remote_copy(
            src_ref=items[wave].at[rows_of(p), both], dst_ref=items[wave].at[rows_of(p + 8), both],
            send_sem=ass.at[wave, d], recv_sem=asr.at[wave, d],
            device_id=sibling, device_id_type=MESH,
        )
        copy.start()
        attending.append(copy)

    def attend_receive(wave, mine):
        mine.wait()
        keys_share(wave, 0)
        for d in range(1, 8):
            here = items[wave].at[rows_of(lax.rem(plane - d + 8, 8)), pl.ds(0, per_head)]
            pltpu.make_async_copy(here, here, ar.at[wave, d]).wait()
            keys_share(wave, d)
        for d in range(8):
            here = items[wave].at[rows_of(lax.rem(plane - d + 8, 8) + 8), both]
            pltpu.make_async_copy(here, here, asr.at[wave, d]).wait()

    def back_view(wave, p):
        start = pl.multiple_of(row * 2 * HDIM + lax.rem(p, 2) * HDIM, 128)
        return heads[wave].at[rows_of(lax.div(p, 2)), pl.ds(start, HDIM)]

    def back(wave, d):
        p = plane_peer(d)
        return pltpu.make_async_remote_copy(
            src_ref=houts[wave].at[rows_of(p)], dst_ref=back_view(wave, plane),
            send_sem=bs.at[wave, d], recv_sem=br.at[wave, d],
            device_id=plane_device(p), device_id_type=MESH,
        )

    power = HDIM ** (-0.5) * 1.4426950408889634

    def attend(wave, d):
        item, rows = items[wave], rows_of(plane_peer(d))
        scores = lax.dot_general(
            item[rows, :HDIM], item[:, HDIM : 2 * HDIM], (((1,), (1,)), ((), ())),
            preferred_element_type=jnp.float32,
        )
        peak = jnp.max(scores, axis=-1, keepdims=True)
        expo = jnp.exp2((scores - peak) * power).astype(jnp.bfloat16)
        mixed = jnp.dot(expo, item[:, 2 * HDIM :], preferred_element_type=jnp.float32)
        houts[wave][rows, :] = (mixed[:, :HDIM] / mixed[:, HDIM:]).astype(jnp.bfloat16)

    def attention(wave):
        for group in range(2):
            order = range(4 * group + 1, 4 * group + 5)
            for d in order:
                attend(wave, d)
            for d in order:
                if d < 8:
                    back(wave, d).start()
        mine = pltpu.make_async_copy(houts[wave].at[rows_of(plane)], back_view(wave, plane), local_sem.at[2])
        mine.start()
        mine.wait()

    def back_receive(wave):
        for d in range(1, 8):
            here = back_view(wave, lax.rem(plane - d + 8, 8))
            pltpu.make_async_copy(here, here, br.at[wave, d]).wait()
        for half in HALVES:
            gh[wave].begin(half)

    mine0 = attend_send(0)
    mine1 = attend_send(1)
    attend_receive(0, mine0)
    attention(0)
    back_receive(0)
    attend_receive(1, mine1)
    for half in HALVES:
        go.begin(half)
    attention(1)
    back_receive(1)

    def near(gather, half):
        for role in (BP, BM, A):
            gather.arrive(role, half)

    near(gh[0], 0)
    near(go, 0)
    near(gh[0], 1)
    near(go, 1)
    gh[0].arrive(D, 0)
    gh[0].arrive(D, 1)
    near(gh[1], 0)
    for half in HALVES:
        go.arrive(CP, half)
        go.arrive(CM, half)
    near(gh[1], 1)
    gh[1].arrive(D, 0)
    gh[1].arrive(D, 1)
    for role in (D, E):
        for half in HALVES:
            go.arrive(role, half)
    for role in range(8):
        go.shared(role)

    def part(wave, role):
        at = pl.multiple_of(gh[wave].block(*gh[wave].place(role)) * 2 * HDIM, 128)
        return jnp.dot(
            heads[wave][:, pl.ds(at, 2 * HDIM)], wobuf[wave, pl.ds(at, 2 * HDIM), :],
            preferred_element_type=jnp.float32,
        )

    def project(*terms):
        total = pacc[...]
        for wave, role in terms:
            total += part(wave, role)
        pacc[...] = total

    pacc[...] = xbuf[:, pl.ds(pl.multiple_of(row * feat, 128), feat)].astype(jnp.float32)
    project((0, OWN), (0, BP), (0, BM), (0, A), (0, D))
    for half in HALVES:
        for role in (CP, CM, E):
            gh[0].arrive(role, half)
    project((0, CP), (0, CM), (0, E), (1, OWN), (1, BP), (1, BM), (1, A), (1, D))
    for half in HALVES:
        for role in (CP, CM, E):
            gh[1].arrive(role, half)
    out_ref[...] = (pacc[...] + part(1, CP) + part(1, CM) + part(1, E)).astype(jnp.bfloat16)

    for gather in (gx, gw, go, *gh):
        gather.finish()
    for copy in told + attending:
        copy.wait_send()
    for wave in range(2):
        for d in range(1, 8):
            back(wave, d).wait_send()


def local(pixels_tokens, ln_gain, ln_bias, w_qkv, w_out):
    images, seq_col, feat = pixels_tokens.shape
    tokens = images * seq_col
    rows, cols = lax.axis_size("row"), lax.axis_size("col")
    bf16, f32 = jnp.bfloat16, jnp.float32
    width = rows * feat
    wcols, ocols = w_qkv.shape[1], w_out.shape[1]
    heads = cols * w_out.shape[0]
    dma = pltpu.SemaphoreType.DMA
    any_space = pl.BlockSpec(memory_space=pl.ANY)
    vmem = pl.BlockSpec(memory_space=pltpu.VMEM)
    pairs = [dma((8, 2)), dma((8, 2))]
    padded = -(-tokens // 128) * 128
    out = pl.pallas_call(
        block_kernel,
        out_shape=jax.ShapeDtypeStruct((tokens, feat), bf16),
        in_specs=[any_space, vmem, vmem, any_space, any_space],
        out_specs=vmem,
        scratch_shapes=[
            pltpu.VMEM((tokens, width), bf16),
            pltpu.VMEM((tokens, width), bf16),
            pltpu.VMEM((width, wcols), bf16),
            pltpu.VMEM((2, heads // 2, ocols), bf16),
            pltpu.VMEM((tokens, wcols), f32),
            pltpu.VMEM((tokens, wcols), bf16),
            pltpu.VMEM((cols * seq_col, 4 * HDIM), bf16),
            pltpu.VMEM((cols * seq_col, 4 * HDIM), bf16),
            pltpu.VMEM((cols * seq_col // 2, HDIM), bf16),
            pltpu.VMEM((cols * seq_col // 2, HDIM), bf16),
            pltpu.VMEM((tokens, heads // 2), bf16),
            pltpu.VMEM((tokens, heads // 2), bf16),
            pltpu.VMEM((tokens, ocols), f32),
            pltpu.VMEM((rows, 8, padded), f32),
            pltpu.VMEM((padded, 128), f32),
            *pairs, *pairs, *pairs, *pairs, *pairs, *pairs, *pairs,
            dma((2, 8)), dma((2, 8)), dma((2, 8)), dma((2, 8)), dma((2, 8)), dma((2, 8)),
            dma((8,)), dma((8,)), dma((4,)),
        ],
        compiler_params=pltpu.CompilerParams(
            collective_id=0, has_side_effects=True, vmem_limit_bytes=61 * 2**20
        ),
        name="attention_block",
    )(pixels_tokens.reshape(tokens, feat), ln_gain.reshape(1, -1), ln_bias.reshape(1, -1), w_qkv, w_out)
    return out.reshape(images, seq_col, feat)


def solution(mesh):
    in_specs = (P(None, "col", "row"), P(), P(), P("col", "row"), P("col", "row"))
    out_specs = P(None, "col", "row")
    return jax.shard_map(local, mesh=mesh, in_specs=in_specs, out_specs=out_specs, check_vma=False)
```

```python
import jax
import jax.numpy as jnp
from jax import lax
from jax.experimental import pallas as pl
from jax.experimental.pallas import tpu as pltpu
from jax.sharding import PartitionSpec as P

HDIM = 128
MESH = pl.DeviceIdType.MESH
HALVES = (0, 1)
OWN, A, BP, BM, CP, CM, D, E = range(8)


def ring(p, step):
    return lax.rem(p + step + 4, 4)


class Gather:
    def __init__(self, p, q, device, block, view, source, sems, last_by_pair, sibling=None):
        self.p, self.q, self.device, self.block = p, q, device, block
        self.view, self.source, self.sems = view, source, sems
        self.last_by_pair, self.sibling = last_by_pair, sibling
        self.sent = []

    def place(self, role):
        p, q, o = self.p, self.q, 1 - self.q
        return {
            OWN: (p, q), A: (p, o), BP: (ring(p, -1), q), BM: (ring(p, 1), q),
            CP: (ring(p, -1), o), CM: (ring(p, 1), o), D: (ring(p, 2), q), E: (ring(p, 2), o),
        }[role]

    def ref(self, role, half):
        return self.view(self.block(*self.place(role)), half)

    def send(self, role, half, there, to):
        send_sem, recv_sem = self.sems[0], self.sems[1]
        src = self.source(half) if role == OWN and self.source is not None else self.ref(role, half)
        copy = pltpu.make_async_remote_copy(
            src_ref=src,
            dst_ref=self.ref(role, half),
            send_sem=send_sem.at[there, half],
            recv_sem=recv_sem.at[there, half],
            device_id=to,
            device_id_type=MESH,
        )
        copy.start()
        self.sent.append(copy)

    def share(self, role, half):
        if self.sibling is None:
            return
        device, view = self.sibling
        send_sem, recv_sem = self.sems[2], self.sems[3]
        src = self.source(half) if role == OWN and self.source is not None else self.ref(role, half)
        copy = pltpu.make_async_remote_copy(
            src_ref=src,
            dst_ref=self.ref(role, half),
            send_sem=send_sem.at[role, half],
            recv_sem=recv_sem.at[role, half],
            device_id=device,
            device_id_type=MESH,
        )
        copy.start()
        self.sent.append(copy)

    def up(self):
        return self.device(ring(self.p, 1), self.q)

    def down(self):
        return self.device(ring(self.p, -1), self.q)

    def across(self):
        return self.device(self.p, 1 - self.q)

    def begin_across(self, half):
        self.send(OWN, half, A, self.across())

    def begin_ring(self, half):
        self.send(OWN, half, BP, self.up())
        self.send(OWN, half, BM, self.down())
        self.share(OWN, half)

    def begin(self, half):
        self.begin_across(half)
        self.begin_ring(half)

    def arrive(self, role, half):
        recv_sem = self.sems[1]
        here = self.ref(role, half)
        pltpu.make_async_copy(here, here, recv_sem.at[role, half]).wait()
        if role == A:
            self.send(A, half, CP, self.up())
            self.send(A, half, CM, self.down())
        elif role == BP and half == 0:
            self.send(BP, half, D, self.up())
        elif role == BM and half == 1:
            self.send(BM, half, D, self.down())
        elif role == D and self.last_by_pair:
            self.send(D, half, E, self.across())
        elif role == CP and half == 0 and not self.last_by_pair:
            self.send(CP, half, E, self.up())
        elif role == CM and half == 1 and not self.last_by_pair:
            self.send(CM, half, E, self.down())
        self.share(role, half)

    def shared(self, role):
        _, view = self.sibling
        for half in HALVES:
            here = view(self.place(role), half)
            pltpu.make_async_copy(here, here, self.sems[3].at[role, half]).wait()

    def finish(self):
        for copy in self.sent:
            copy.wait_send()


def block_kernel(
    x_ref, gain_ref, bias_ref, wq_ref, wo_ref, out_ref,
    xbuf, nbuf, wbuf, wobuf, acc, qkv, item0, item1, hout0, hout1, heads0, heads1, pacc,
    stats, moments,
    xs, xr, ws, wr, wss, wsr, os, orr, oss, osr, hs0, hr0, hs1, hr1,
    as_, ar, ass, asr, bs, br, ms, mr, local_sem,
):
    row, col = lax.axis_index("row"), lax.axis_index("col")
    zh, xx = lax.div(row, 4), lax.rem(row, 4)
    yy, zl, core = lax.div(col, 4), lax.rem(lax.div(col, 2), 2), lax.rem(col, 2)
    plane = lax.div(col, 2)
    tokens, feat = x_ref.shape
    wrows, wcols = wq_ref.shape
    orows, ocols = wo_ref.shape
    seq_col = tokens // 4
    per_head = 3 * HDIM
    items, houts, heads = (item0, item1), (hout0, hout1), (heads0, heads1)
    sibling = (row, plane * 2 + 1 - core)

    def col_device(y, z):
        return (row, y * 4 + z * 2 + core)

    def row_device(x, h):
        return (h * 4 + x, col)

    def plane_peer(d):
        return lax.rem(plane + d, 8)

    def plane_device(p):
        return (row, p * 2 + core)

    def row_peer(d):
        return (lax.rem(row + d, 8), col)

    barrier = pltpu.get_barrier_semaphore()
    for d in range(1, 8):
        pl.semaphore_signal(barrier, inc=1, device_id=plane_device(plane_peer(d)), device_id_type=MESH)
        pl.semaphore_signal(barrier, inc=1, device_id=row_peer(d), device_id_type=MESH)
    pl.semaphore_signal(barrier, inc=1, device_id=sibling, device_id_type=MESH)

    def cols(ref, start, size, rows=None):
        rows = pl.ds(0, tokens) if rows is None else rows
        return ref.at[rows, pl.ds(pl.multiple_of(start, 128), size)]

    half_rows = wrows // 2

    def wq_view(k):
        def view(place, half):
            start = (place[0] * 4 + place[1] * 2 + k) * wrows + half * half_rows
            return wbuf.at[pl.ds(pl.multiple_of(start, 16), half_rows)]

        return view

    def wo_view(k):
        def view(place, half):
            start = (place[0] * 4 + place[1] * 2 + k) * HDIM
            return wobuf.at[half, pl.ds(pl.multiple_of(start, 16), HDIM)]

        return view

    def weight_gather(src, view, sems, last_by_pair):
        size = src.shape[0] // 2
        return Gather(
            yy, zl, col_device, lambda y, z: (y, z), view(core),
            lambda half: src.at[pl.ds(half * size, size)], sems, last_by_pair,
            sibling=(sibling, view(1 - core)),
        )

    half_tokens = tokens // 2

    def row_gather(buf, width, source, sems, last_by_pair):
        return Gather(
            xx, zh, row_device, lambda x, h: h * 4 + x,
            lambda b, half: cols(buf, b * width, width, pl.ds(half * half_tokens, half_tokens)),
            source, sems, last_by_pair,
        )

    gx = row_gather(xbuf, feat, lambda half: x_ref.at[pl.ds(half * half_tokens, half_tokens)], (xs, xr), False)
    gw = weight_gather(wq_ref, wq_view, (ws, wr, wss, wsr), True)
    go = weight_gather(wo_ref, wo_view, (os, orr, oss, osr), False)
    gh = [
        row_gather(heads0, 2 * HDIM, None, (hs0, hr0), True),
        row_gather(heads1, 2 * HDIM, None, (hs1, hr1), True),
    ]

    own = [
        pltpu.make_async_copy(x_ref, cols(xbuf, row * feat, feat), local_sem.at[0]),
        pltpu.make_async_copy(wq_ref, wbuf.at[pl.ds(pl.multiple_of(col * wrows, 16), wrows)], local_sem.at[1]),
        pltpu.make_async_copy(wo_ref.at[pl.ds(0, HDIM)], wo_view(core)((yy, zl), 0), local_sem.at[2]),
        pltpu.make_async_copy(wo_ref.at[pl.ds(HDIM, HDIM)], wo_view(core)((yy, zl), 1), local_sem.at[3]),
    ]
    for copy in own:
        copy.start()
    pl.semaphore_wait(barrier, 15)

    for half in HALVES:
        gx.begin(half)
        gw.begin_ring(half)
    for copy in own:
        copy.wait()

    chunk = 96
    means, rates = moments.at[0], moments.at[1]
    padded = moments.shape[1]
    means[...] = jnp.zeros_like(means)

    @pl.loop(0, tokens // chunk)
    def _(i):
        rows = pl.ds(pl.multiple_of(i * chunk, chunk), chunk)
        floats = xbuf[rows, pl.ds(pl.multiple_of(row * feat, 128), feat)].astype(jnp.float32)
        center = jnp.sum(floats, axis=-1, keepdims=True) * (1.0 / feat)
        moved = floats - center
        square = jnp.sum(moved * moved, axis=-1, keepdims=True)
        lane = lax.broadcasted_iota(jnp.int32, (chunk, 128), 1)
        means[rows, :] = jnp.where(lane == 0, center, jnp.where(lane == 1, square, 0.0))

    stats[row] = means[...].T[:8]
    told = []
    for d in range(1, 8):
        copy = pltpu.make_async_remote_copy(
            src_ref=stats.at[row], dst_ref=stats.at[row], send_sem=ms.at[d], recv_sem=mr.at[d],
            device_id=row_peer(d), device_id_type=MESH,
        )
        copy.start()
        told.append(copy)
    for item in items:
        item[:, 3 * HDIM :] = jnp.ones((item.shape[0], HDIM), jnp.bfloat16)

    gx.arrive(A, 0)
    gw.begin_across(0)
    gx.arrive(BP, 0)
    gx.arrive(BM, 0)
    for d in range(1, 8):
        here = stats.at[lax.rem(row - d + 8, 8)]
        pltpu.make_async_copy(here, here, mr.at[d]).wait()
    centers = stats[:, 0, :]
    mean = jnp.sum(centers, axis=0, keepdims=True) * (1.0 / 8)
    off = centers - mean
    square = jnp.sum(stats[:, 1, :], axis=0, keepdims=True) + jnp.sum(off * off, axis=0, keepdims=True) * feat
    rate = lax.rsqrt(square * (1.0 / (8 * feat)) + 1e-06)
    means[...] = jnp.broadcast_to(mean, (128, padded)).T
    rates[...] = jnp.broadcast_to(rate, (128, padded)).T

    def normalise(role):
        start = gx.block(*gx.place(role)) * feat

        @pl.loop(0, tokens // chunk)
        def _(i):
            rows = pl.ds(pl.multiple_of(i * chunk, chunk), chunk)
            mean, rate = means[rows, :], rates[rows, :]
            for step in range(feat // 128):
                columns = pl.ds(pl.multiple_of(start + step * 128, 128), 128)
                floats = xbuf[rows, columns].astype(jnp.float32)
                nbuf[rows, columns] = (
                    (floats - mean) * rate * gain_ref[:, columns] + bias_ref[:, columns]
                ).astype(jnp.bfloat16)

    normalise(OWN)
    gw.arrive(BP, 0)
    gw.arrive(BM, 0)
    gx.arrive(A, 1)
    gw.begin_across(1)
    gx.arrive(BP, 1)
    gx.arrive(BM, 1)
    normalise(A)
    normalise(BP)
    normalise(BM)
    gw.arrive(BP, 1)
    gw.arrive(BM, 1)
    gw.arrive(A, 0)
    gx.arrive(CP, 0)
    gx.arrive(CM, 0)
    gw.arrive(D, 0)
    gw.arrive(D, 1)
    gw.arrive(A, 1)
    gx.arrive(CP, 1)
    gx.arrive(CM, 1)
    normalise(CP)
    normalise(CM)
    gx.arrive(D, 0)
    gx.arrive(D, 1)
    normalise(D)
    gx.arrive(E, 0)
    gx.arrive(E, 1)
    normalise(E)

    unit = 2 * wrows

    def product(place, columns):
        at = pl.multiple_of((place[0] * 2 + place[1]) * unit, 128)
        return jnp.dot(
            nbuf[:, pl.ds(at, unit)], wbuf[pl.ds(at, unit), columns], preferred_element_type=jnp.float32
        )

    def multiply(role, first=False):
        gw.shared(role)
        place = gw.place(role)

        @pl.loop(0, wcols // per_head)
        def _(j):
            columns = pl.ds(pl.multiple_of(j * per_head, 128), per_head)
            if first:
                acc[:, columns] = product(place, columns)
            else:
                acc[:, columns] += product(place, columns)

    multiply(OWN, first=True)
    multiply(BP)
    multiply(BM)
    multiply(A)
    gw.arrive(CP, 0)
    gw.arrive(CM, 0)
    multiply(D)
    gw.arrive(E, 0)
    gw.arrive(CP, 1)
    gw.arrive(CM, 1)
    gw.arrive(E, 1)
    for role in (CP, CM, E):
        gw.shared(role)

    def rows_of(p):
        return pl.ds(pl.multiple_of(p * seq_col, 16), seq_col)

    def to_attend(wave, d):
        p = plane_peer(d)
        start = pl.multiple_of((lax.rem(p, 2) * 2 + wave) * per_head, 128)
        src = qkv.at[rows_of(lax.div(p, 2)), pl.ds(start, per_head)]
        dst = items[wave].at[rows_of(plane), pl.ds(0, per_head)]
        return src, dst, plane_device(p)

    attending = []

    def complete(wave):
        for z in range(2):
            columns = pl.ds((z * 2 + wave) * per_head, per_head)
            total = acc[:, columns]
            for role in (CP, CM, E):
                total += product(gw.place(role), columns)
            qkv[:, columns] = total.astype(jnp.bfloat16)

    def attend_send(wave):
        src, dst, _ = to_attend(wave, 0)
        mine = pltpu.make_async_copy(src, dst, local_sem.at[wave])
        mine.start()
        for d in range(1, 8):
            src, dst, device = to_attend(wave, d)
            copy = pltpu.make_async_remote_copy(
                src_ref=src, dst_ref=dst, send_sem=as_.at[wave, d], recv_sem=ar.at[wave, d],
                device_id=device, device_id_type=MESH,
            )
            copy.start()
            attending.append(copy)
        return mine

    both = pl.ds(HDIM, 2 * HDIM)

    def keys_share(wave, d):
        p = lax.rem(plane - d + 8, 8)
        copy = pltpu.make_async_remote_copy(
            src_ref=items[wave].at[rows_of(p), both], dst_ref=items[wave].at[rows_of(p + 8), both],
            send_sem=ass.at[wave, d], recv_sem=asr.at[wave, d],
            device_id=sibling, device_id_type=MESH,
        )
        copy.start()
        attending.append(copy)

    def attend_receive(wave, mine):
        mine.wait()
        keys_share(wave, 0)
        for d in range(1, 8):
            here = items[wave].at[rows_of(lax.rem(plane - d + 8, 8)), pl.ds(0, per_head)]
            pltpu.make_async_copy(here, here, ar.at[wave, d]).wait()
            keys_share(wave, d)
        for d in range(8):
            here = items[wave].at[rows_of(lax.rem(plane - d + 8, 8) + 8), both]
            pltpu.make_async_copy(here, here, asr.at[wave, d]).wait()

    def back_view(wave, p):
        start = pl.multiple_of(row * 2 * HDIM + lax.rem(p, 2) * HDIM, 128)
        return heads[wave].at[rows_of(lax.div(p, 2)), pl.ds(start, HDIM)]

    def back(wave, d):
        p = plane_peer(d)
        return pltpu.make_async_remote_copy(
            src_ref=houts[wave].at[rows_of(p)], dst_ref=back_view(wave, plane),
            send_sem=bs.at[wave, d], recv_sem=br.at[wave, d],
            device_id=plane_device(p), device_id_type=MESH,
        )

    power = HDIM ** (-0.5) * 1.4426950408889634

    def attend(wave, d):
        item, rows = items[wave], rows_of(plane_peer(d))
        scores = lax.dot_general(
            item[rows, :HDIM], item[:, HDIM : 2 * HDIM], (((1,), (1,)), ((), ())),
            preferred_element_type=jnp.float32,
        )
        peak = jnp.max(scores, axis=-1, keepdims=True)
        expo = jnp.exp2((scores - peak) * power).astype(jnp.bfloat16)
        mixed = jnp.dot(expo, item[:, 2 * HDIM :], preferred_element_type=jnp.float32)
        houts[wave][rows, :] = (mixed[:, :HDIM] / mixed[:, HDIM:]).astype(jnp.bfloat16)

    def attention(wave, group):
        order = range(4 * group + 1, 4 * group + 5)
        for d in order:
            attend(wave, d)
        for d in order:
            if d < 8:
                back(wave, d).start()
            else:
                mine = pltpu.make_async_copy(houts[wave].at[rows_of(plane)], back_view(wave, plane), local_sem.at[2])
                mine.start()
                mine.wait()

    def back_receive(wave):
        for d in range(1, 8):
            here = back_view(wave, lax.rem(plane - d + 8, 8))
            pltpu.make_async_copy(here, here, br.at[wave, d]).wait()
        for half in HALVES:
            gh[wave].begin(half)

    def near(gather, half):
        for role in (BP, BM, A):
            gather.arrive(role, half)

    complete(0)
    mine0 = attend_send(0)
    complete(1)
    attend_receive(0, mine0)
    mine1 = attend_send(1)
    attention(0, 0)
    attention(0, 1)
    back_receive(0)
    attend_receive(1, mine1)
    for half in HALVES:
        go.begin(half)
    attention(1, 0)
    near(gh[0], 0)
    attention(1, 1)
    near(gh[0], 1)
    back_receive(1)

    gh[0].arrive(D, 0)
    gh[0].arrive(D, 1)
    near(go, 0)
    near(go, 1)
    near(gh[1], 0)
    for half in HALVES:
        go.arrive(CP, half)
        go.arrive(CM, half)
    near(gh[1], 1)
    gh[1].arrive(D, 0)
    gh[1].arrive(D, 1)
    for role in (D, E):
        for half in HALVES:
            go.arrive(role, half)
    for role in range(8):
        go.shared(role)

    def part(wave, role):
        at = pl.multiple_of(gh[wave].block(*gh[wave].place(role)) * 2 * HDIM, 128)
        return jnp.dot(
            heads[wave][:, pl.ds(at, 2 * HDIM)], wobuf[wave, pl.ds(at, 2 * HDIM), :],
            preferred_element_type=jnp.float32,
        )

    def project(*terms):
        total = pacc[...]
        for wave, role in terms:
            total += part(wave, role)
        pacc[...] = total

    pacc[...] = xbuf[:, pl.ds(pl.multiple_of(row * feat, 128), feat)].astype(jnp.float32)
    project((0, OWN), (0, BP), (0, BM), (0, A), (0, D))
    for half in HALVES:
        for role in (CP, CM, E):
            gh[0].arrive(role, half)
    project((0, CP), (0, CM), (0, E), (1, OWN), (1, BP), (1, BM), (1, A), (1, D))
    for half in HALVES:
        for role in (CP, CM, E):
            gh[1].arrive(role, half)
    out_ref[...] = (pacc[...] + part(1, CP) + part(1, CM) + part(1, E)).astype(jnp.bfloat16)

    for gather in (gx, gw, go, *gh):
        gather.finish()
    for copy in told + attending:
        copy.wait_send()
    for wave in range(2):
        for d in range(1, 8):
            back(wave, d).wait_send()


def local(pixels_tokens, ln_gain, ln_bias, w_qkv, w_out):
    images, seq_col, feat = pixels_tokens.shape
    tokens = images * seq_col
    rows, cols = lax.axis_size("row"), lax.axis_size("col")
    bf16, f32 = jnp.bfloat16, jnp.float32
    width = rows * feat
    wcols, ocols = w_qkv.shape[1], w_out.shape[1]
    heads = cols * w_out.shape[0]
    dma = pltpu.SemaphoreType.DMA
    any_space = pl.BlockSpec(memory_space=pl.ANY)
    vmem = pl.BlockSpec(memory_space=pltpu.VMEM)
    pairs = [dma((8, 2)), dma((8, 2))]
    padded = -(-tokens // 128) * 128
    out = pl.pallas_call(
        block_kernel,
        out_shape=jax.ShapeDtypeStruct((tokens, feat), bf16),
        in_specs=[any_space, vmem, vmem, any_space, any_space],
        out_specs=vmem,
        scratch_shapes=[
            pltpu.VMEM((tokens, width), bf16),
            pltpu.VMEM((tokens, width), bf16),
            pltpu.VMEM((width, wcols), bf16),
            pltpu.VMEM((2, heads // 2, ocols), bf16),
            pltpu.VMEM((tokens, wcols), f32),
            pltpu.VMEM((tokens, wcols), bf16),
            pltpu.VMEM((cols * seq_col, 4 * HDIM), bf16),
            pltpu.VMEM((cols * seq_col, 4 * HDIM), bf16),
            pltpu.VMEM((cols * seq_col // 2, HDIM), bf16),
            pltpu.VMEM((cols * seq_col // 2, HDIM), bf16),
            pltpu.VMEM((tokens, heads // 2), bf16),
            pltpu.VMEM((tokens, heads // 2), bf16),
            pltpu.VMEM((tokens, ocols), f32),
            pltpu.VMEM((rows, 8, padded), f32),
            pltpu.VMEM((2, padded, 128), f32),
            *pairs, *pairs, *pairs, *pairs, *pairs, *pairs, *pairs,
            dma((2, 8)), dma((2, 8)), dma((2, 8)), dma((2, 8)), dma((2, 8)), dma((2, 8)),
            dma((8,)), dma((8,)), dma((4,)),
        ],
        compiler_params=pltpu.CompilerParams(
            collective_id=0, has_side_effects=True, vmem_limit_bytes=61 * 2**20
        ),
        name="attention_block",
    )(pixels_tokens.reshape(tokens, feat), ln_gain.reshape(1, -1), ln_bias.reshape(1, -1), w_qkv, w_out)
    return out.reshape(images, seq_col, feat)


def solution(mesh):
    in_specs = (P(None, "col", "row"), P(), P(), P("col", "row"), P("col", "row"))
    out_specs = P(None, "col", "row")
    return jax.shard_map(local, mesh=mesh, in_specs=in_specs, out_specs=out_specs, check_vma=False)
```

```python
import jax
import jax.numpy as jnp
from jax import lax
from jax.experimental import pallas as pl
from jax.experimental.pallas import tpu as pltpu
from jax.sharding import PartitionSpec as P

HDIM = 128
MESH = pl.DeviceIdType.MESH
HALVES = (0, 1)
OWN, A, BP, BM, CP, CM, D, E = range(8)


def ring(p, step):
    return lax.rem(p + step + 4, 4)


class Gather:
    def __init__(self, p, q, device, block, view, source, sems, last_by_pair, sibling=None):
        self.p, self.q, self.device, self.block = p, q, device, block
        self.view, self.source, self.sems = view, source, sems
        self.last_by_pair, self.sibling = last_by_pair, sibling
        self.sent = []

    def place(self, role):
        p, q, o = self.p, self.q, 1 - self.q
        return {
            OWN: (p, q), A: (p, o), BP: (ring(p, -1), q), BM: (ring(p, 1), q),
            CP: (ring(p, -1), o), CM: (ring(p, 1), o), D: (ring(p, 2), q), E: (ring(p, 2), o),
        }[role]

    def ref(self, role, half):
        return self.view(self.block(*self.place(role)), half)

    def send(self, role, half, there, to):
        send_sem, recv_sem = self.sems[0], self.sems[1]
        src = self.source(half) if role == OWN and self.source is not None else self.ref(role, half)
        copy = pltpu.make_async_remote_copy(
            src_ref=src,
            dst_ref=self.ref(role, half),
            send_sem=send_sem.at[there, half],
            recv_sem=recv_sem.at[there, half],
            device_id=to,
            device_id_type=MESH,
        )
        copy.start()
        self.sent.append(copy)

    def share(self, role, half):
        if self.sibling is None:
            return
        device, view = self.sibling
        send_sem, recv_sem = self.sems[2], self.sems[3]
        src = self.source(half) if role == OWN and self.source is not None else self.ref(role, half)
        copy = pltpu.make_async_remote_copy(
            src_ref=src,
            dst_ref=self.ref(role, half),
            send_sem=send_sem.at[role, half],
            recv_sem=recv_sem.at[role, half],
            device_id=device,
            device_id_type=MESH,
        )
        copy.start()
        self.sent.append(copy)

    def up(self):
        return self.device(ring(self.p, 1), self.q)

    def down(self):
        return self.device(ring(self.p, -1), self.q)

    def across(self):
        return self.device(self.p, 1 - self.q)

    def begin_across(self, half):
        self.send(OWN, half, A, self.across())

    def begin_ring(self, half):
        self.send(OWN, half, BP, self.up())
        self.send(OWN, half, BM, self.down())
        self.share(OWN, half)

    def begin(self, half):
        self.begin_across(half)
        self.begin_ring(half)

    def arrive(self, role, half):
        recv_sem = self.sems[1]
        here = self.ref(role, half)
        pltpu.make_async_copy(here, here, recv_sem.at[role, half]).wait()
        if role == A:
            self.send(A, half, CP, self.up())
            self.send(A, half, CM, self.down())
        elif role == BP and half == 0:
            self.send(BP, half, D, self.up())
        elif role == BM and half == 1:
            self.send(BM, half, D, self.down())
        elif role == D and self.last_by_pair:
            self.send(D, half, E, self.across())
        elif role == CP and half == 0 and not self.last_by_pair:
            self.send(CP, half, E, self.up())
        elif role == CM and half == 1 and not self.last_by_pair:
            self.send(CM, half, E, self.down())
        self.share(role, half)

    def shared(self, role):
        _, view = self.sibling
        for half in HALVES:
            here = view(self.place(role), half)
            pltpu.make_async_copy(here, here, self.sems[3].at[role, half]).wait()

    def finish(self):
        for copy in self.sent:
            copy.wait_send()


def block_kernel(
    x_ref, gain_ref, bias_ref, wq_ref, wo_ref, out_ref,
    xbuf, nbuf, wbuf, wobuf, acc, qkv, item0, item1, hout0, hout1, heads0, heads1, pacc,
    stats, moments,
    xs, xr, ws, wr, wss, wsr, os, orr, oss, osr, hs0, hr0, hs1, hr1,
    as_, ar, ass, asr, bs, br, ms, mr, local_sem,
):
    row, col = lax.axis_index("row"), lax.axis_index("col")
    zh, xx = lax.div(row, 4), lax.rem(row, 4)
    yy, zl, core = lax.div(col, 4), lax.rem(lax.div(col, 2), 2), lax.rem(col, 2)
    plane = lax.div(col, 2)
    tokens, feat = x_ref.shape
    wrows, wcols = wq_ref.shape
    orows, ocols = wo_ref.shape
    seq_col = tokens // 4
    per_head = 3 * HDIM
    items, houts, heads = (item0, item1), (hout0, hout1), (heads0, heads1)
    sibling = (row, plane * 2 + 1 - core)

    def col_device(y, z):
        return (row, y * 4 + z * 2 + core)

    def row_device(x, h):
        return (h * 4 + x, col)

    def plane_peer(d):
        return lax.rem(plane + d, 8)

    def plane_device(p):
        return (row, p * 2 + core)

    def row_peer(d):
        return (lax.rem(row + d, 8), col)

    barrier = pltpu.get_barrier_semaphore()
    for d in range(1, 8):
        pl.semaphore_signal(barrier, inc=1, device_id=plane_device(plane_peer(d)), device_id_type=MESH)
        pl.semaphore_signal(barrier, inc=1, device_id=row_peer(d), device_id_type=MESH)
    pl.semaphore_signal(barrier, inc=1, device_id=sibling, device_id_type=MESH)

    def cols(ref, start, size, rows=None):
        rows = pl.ds(0, tokens) if rows is None else rows
        return ref.at[rows, pl.ds(pl.multiple_of(start, 128), size)]

    half_rows = wrows // 2

    def wq_view(k):
        def view(place, half):
            start = (place[0] * 4 + place[1] * 2 + k) * wrows + half * half_rows
            return wbuf.at[pl.ds(pl.multiple_of(start, 16), half_rows)]

        return view

    def wo_view(k):
        def view(place, half):
            start = (place[0] * 4 + place[1] * 2 + k) * HDIM
            return wobuf.at[half, pl.ds(pl.multiple_of(start, 16), HDIM)]

        return view

    def weight_gather(src, view, sems, last_by_pair):
        size = src.shape[0] // 2
        return Gather(
            yy, zl, col_device, lambda y, z: (y, z), view(core),
            lambda half: src.at[pl.ds(half * size, size)], sems, last_by_pair,
            sibling=(sibling, view(1 - core)),
        )

    half_tokens = tokens // 2

    def row_gather(buf, width, source, sems, last_by_pair):
        return Gather(
            xx, zh, row_device, lambda x, h: h * 4 + x,
            lambda b, half: cols(buf, b * width, width, pl.ds(half * half_tokens, half_tokens)),
            source, sems, last_by_pair,
        )

    gx = row_gather(xbuf, feat, lambda half: x_ref.at[pl.ds(half * half_tokens, half_tokens)], (xs, xr), False)
    gw = weight_gather(wq_ref, wq_view, (ws, wr, wss, wsr), True)
    go = weight_gather(wo_ref, wo_view, (os, orr, oss, osr), False)
    gh = [
        row_gather(heads0, 2 * HDIM, None, (hs0, hr0), True),
        row_gather(heads1, 2 * HDIM, None, (hs1, hr1), True),
    ]

    own = [
        pltpu.make_async_copy(x_ref, cols(xbuf, row * feat, feat), local_sem.at[0]),
        pltpu.make_async_copy(wq_ref, wbuf.at[pl.ds(pl.multiple_of(col * wrows, 16), wrows)], local_sem.at[1]),
        pltpu.make_async_copy(wo_ref.at[pl.ds(0, HDIM)], wo_view(core)((yy, zl), 0), local_sem.at[2]),
        pltpu.make_async_copy(wo_ref.at[pl.ds(HDIM, HDIM)], wo_view(core)((yy, zl), 1), local_sem.at[3]),
    ]
    for copy in own:
        copy.start()
    pl.semaphore_wait(barrier, 15)

    for half in HALVES:
        gx.begin(half)
        gw.begin_ring(half)
    for copy in own:
        copy.wait()

    chunk = 96
    means, rates = moments.at[0], moments.at[1]
    padded = moments.shape[1]
    means[...] = jnp.zeros_like(means)

    @pl.loop(0, tokens // chunk)
    def _(i):
        rows = pl.ds(pl.multiple_of(i * chunk, chunk), chunk)
        floats = xbuf[rows, pl.ds(pl.multiple_of(row * feat, 128), feat)].astype(jnp.float32)
        center = jnp.sum(floats, axis=-1, keepdims=True) * (1.0 / feat)
        moved = floats - center
        square = jnp.sum(moved * moved, axis=-1, keepdims=True)
        lane = lax.broadcasted_iota(jnp.int32, (chunk, 128), 1)
        means[rows, :] = jnp.where(lane == 0, center, jnp.where(lane == 1, square, 0.0))

    stats[row] = means[...].T[:8]
    told = []
    for d in range(1, 8):
        copy = pltpu.make_async_remote_copy(
            src_ref=stats.at[row], dst_ref=stats.at[row], send_sem=ms.at[d], recv_sem=mr.at[d],
            device_id=row_peer(d), device_id_type=MESH,
        )
        copy.start()
        told.append(copy)
    for item in items:
        item[:, 3 * HDIM :] = jnp.ones((item.shape[0], HDIM), jnp.bfloat16)

    gx.arrive(A, 0)
    gw.begin_across(0)
    gx.arrive(BP, 0)
    gx.arrive(BM, 0)
    for d in range(1, 8):
        here = stats.at[lax.rem(row - d + 8, 8)]
        pltpu.make_async_copy(here, here, mr.at[d]).wait()
    centers = stats[:, 0, :]
    mean = jnp.sum(centers, axis=0, keepdims=True) * (1.0 / 8)
    off = centers - mean
    square = jnp.sum(stats[:, 1, :], axis=0, keepdims=True) + jnp.sum(off * off, axis=0, keepdims=True) * feat
    rate = lax.rsqrt(square * (1.0 / (8 * feat)) + 1e-06)
    means[...] = jnp.broadcast_to(mean, (128, padded)).T
    rates[...] = jnp.broadcast_to(rate, (128, padded)).T

    def normalise(role):
        start = gx.block(*gx.place(role)) * feat

        @pl.loop(0, tokens // chunk)
        def _(i):
            rows = pl.ds(pl.multiple_of(i * chunk, chunk), chunk)
            mean, rate = means[rows, :], rates[rows, :]
            for step in range(feat // 128):
                columns = pl.ds(pl.multiple_of(start + step * 128, 128), 128)
                floats = xbuf[rows, columns].astype(jnp.float32)
                nbuf[rows, columns] = (
                    (floats - mean) * rate * gain_ref[:, columns] + bias_ref[:, columns]
                ).astype(jnp.bfloat16)

    normalise(OWN)
    gw.arrive(BP, 0)
    gw.arrive(BM, 0)
    gx.arrive(A, 1)
    gw.begin_across(1)
    gx.arrive(BP, 1)
    gx.arrive(BM, 1)
    normalise(A)
    normalise(BP)
    normalise(BM)
    gw.arrive(BP, 1)
    gw.arrive(BM, 1)
    gw.arrive(A, 0)
    gx.arrive(CP, 0)
    gx.arrive(CM, 0)
    gw.arrive(D, 0)
    gw.arrive(D, 1)
    gw.arrive(A, 1)
    gx.arrive(CP, 1)
    gx.arrive(CM, 1)
    normalise(CP)
    normalise(CM)
    gx.arrive(D, 0)
    gx.arrive(D, 1)
    normalise(D)
    gx.arrive(E, 0)
    gx.arrive(E, 1)
    normalise(E)

    unit = 2 * wrows

    def product(place, columns):
        at = pl.multiple_of((place[0] * 2 + place[1]) * unit, 128)
        return jnp.dot(
            nbuf[:, pl.ds(at, unit)], wbuf[pl.ds(at, unit), columns], preferred_element_type=jnp.float32
        )

    def multiply(role, first=False):
        gw.shared(role)
        place = gw.place(role)

        @pl.loop(0, wcols // 256)
        def _(j):
            columns = pl.ds(pl.multiple_of(j * 256, 256), 256)
            if first:
                acc[:, columns] = product(place, columns)
            else:
                acc[:, columns] += product(place, columns)

    multiply(OWN, first=True)
    multiply(BP)
    multiply(BM)
    multiply(A)
    gw.arrive(CP, 0)
    gw.arrive(CM, 0)
    multiply(D)
    gw.arrive(E, 0)
    gw.arrive(CP, 1)
    gw.arrive(CM, 1)
    gw.arrive(E, 1)
    for half in HALVES:
        go.begin_across(half)
    for role in (CP, CM, E):
        gw.shared(role)

    def rows_of(p):
        return pl.ds(pl.multiple_of(p * seq_col, 16), seq_col)

    def to_attend(wave, d):
        p = plane_peer(d)
        start = pl.multiple_of((lax.rem(p, 2) * 2 + wave) * per_head, 128)
        src = qkv.at[rows_of(lax.div(p, 2)), pl.ds(start, per_head)]
        dst = items[wave].at[rows_of(plane), pl.ds(0, per_head)]
        return src, dst, plane_device(p)

    attending = []

    def complete(wave):
        for z in range(2):
            columns = pl.ds((z * 2 + wave) * per_head, per_head)
            total = acc[:, columns]
            for role in (CP, CM, E):
                total += product(gw.place(role), columns)
            qkv[:, columns] = total.astype(jnp.bfloat16)

    def attend_send(wave):
        src, dst, _ = to_attend(wave, 0)
        mine = pltpu.make_async_copy(src, dst, local_sem.at[wave])
        mine.start()
        for d in range(1, 8):
            src, dst, device = to_attend(wave, d)
            copy = pltpu.make_async_remote_copy(
                src_ref=src, dst_ref=dst, send_sem=as_.at[wave, d], recv_sem=ar.at[wave, d],
                device_id=device, device_id_type=MESH,
            )
            copy.start()
            attending.append(copy)
        return mine

    both = pl.ds(HDIM, 2 * HDIM)

    def keys_share(wave, d):
        p = lax.rem(plane - d + 8, 8)
        copy = pltpu.make_async_remote_copy(
            src_ref=items[wave].at[rows_of(p), both], dst_ref=items[wave].at[rows_of(p + 8), both],
            send_sem=ass.at[wave, d], recv_sem=asr.at[wave, d],
            device_id=sibling, device_id_type=MESH,
        )
        copy.start()
        attending.append(copy)

    def attend_receive(wave, mine):
        mine.wait()
        keys_share(wave, 0)
        for d in range(1, 8):
            here = items[wave].at[rows_of(lax.rem(plane - d + 8, 8)), pl.ds(0, per_head)]
            pltpu.make_async_copy(here, here, ar.at[wave, d]).wait()
            keys_share(wave, d)
        for d in range(8):
            here = items[wave].at[rows_of(lax.rem(plane - d + 8, 8) + 8), both]
            pltpu.make_async_copy(here, here, asr.at[wave, d]).wait()

    def back_view(wave, p):
        start = pl.multiple_of(row * 2 * HDIM + lax.rem(p, 2) * HDIM, 128)
        return heads[wave].at[rows_of(lax.div(p, 2)), pl.ds(start, HDIM)]

    def back(wave, d):
        p = plane_peer(d)
        return pltpu.make_async_remote_copy(
            src_ref=houts[wave].at[rows_of(p)], dst_ref=back_view(wave, plane),
            send_sem=bs.at[wave, d], recv_sem=br.at[wave, d],
            device_id=plane_device(p), device_id_type=MESH,
        )

    power = HDIM ** (-0.5) * 1.4426950408889634

    def attend(wave, d):
        item, rows = items[wave], rows_of(plane_peer(d))
        scores = lax.dot_general(
            item[rows, :HDIM], item[:, HDIM : 2 * HDIM], (((1,), (1,)), ((), ())),
            preferred_element_type=jnp.float32,
        )
        peak = jnp.max(scores, axis=-1, keepdims=True)
        expo = jnp.exp2((scores - peak) * power).astype(jnp.bfloat16)
        mixed = jnp.dot(expo, item[:, 2 * HDIM :], preferred_element_type=jnp.float32)
        houts[wave][rows, :] = (mixed[:, :HDIM] / mixed[:, HDIM:]).astype(jnp.bfloat16)

    def attention(wave, group):
        order = range(4 * group + 1, 4 * group + 5)
        for d in order:
            attend(wave, d)
        for d in order:
            if d < 8:
                back(wave, d).start()
            else:
                mine = pltpu.make_async_copy(houts[wave].at[rows_of(plane)], back_view(wave, plane), local_sem.at[2])
                mine.start()
                mine.wait()

    def back_receive(wave):
        for d in range(1, 8):
            here = back_view(wave, lax.rem(plane - d + 8, 8))
            pltpu.make_async_copy(here, here, br.at[wave, d]).wait()
        for half in HALVES:
            gh[wave].begin(half)

    def near(gather, half):
        for role in (BP, BM, A):
            gather.arrive(role, half)

    complete(0)
    mine0 = attend_send(0)
    complete(1)
    attend_receive(0, mine0)
    mine1 = attend_send(1)
    attention(0, 0)
    attention(0, 1)
    for half in HALVES:
        go.begin_ring(half)
    back_receive(0)
    attend_receive(1, mine1)
    attention(1, 0)
    near(gh[0], 0)
    near(go, 0)
    near(go, 1)
    attention(1, 1)
    near(gh[0], 1)
    gh[0].arrive(D, 0)
    gh[0].arrive(D, 1)
    back_receive(1)

    for half in HALVES:
        go.arrive(CP, half)
        go.arrive(CM, half)
    for half in HALVES:
        go.arrive(D, half)
    near(gh[1], 0)
    near(gh[1], 1)
    for half in HALVES:
        go.arrive(E, half)
    gh[1].arrive(D, 0)
    gh[1].arrive(D, 1)
    for role in range(8):
        go.shared(role)

    def part(wave, role):
        at = pl.multiple_of(gh[wave].block(*gh[wave].place(role)) * 2 * HDIM, 128)
        return jnp.dot(
            heads[wave][:, pl.ds(at, 2 * HDIM)], wobuf[wave, pl.ds(at, 2 * HDIM), :],
            preferred_element_type=jnp.float32,
        )

    def project(*terms):
        total = pacc[...]
        for wave, role in terms:
            total += part(wave, role)
        pacc[...] = total

    pacc[...] = xbuf[:, pl.ds(pl.multiple_of(row * feat, 128), feat)].astype(jnp.float32)
    project((0, OWN), (0, BP), (0, BM), (0, A), (0, D))
    for half in HALVES:
        for role in (CP, CM, E):
            gh[0].arrive(role, half)
    project((0, CP), (0, CM), (0, E), (1, OWN), (1, BP), (1, BM), (1, A), (1, D))
    for half in HALVES:
        for role in (CP, CM, E):
            gh[1].arrive(role, half)
    out_ref[...] = (pacc[...] + part(1, CP) + part(1, CM) + part(1, E)).astype(jnp.bfloat16)

    for gather in (gx, gw, go, *gh):
        gather.finish()
    for copy in told + attending:
        copy.wait_send()
    for wave in range(2):
        for d in range(1, 8):
            back(wave, d).wait_send()


def local(pixels_tokens, ln_gain, ln_bias, w_qkv, w_out):
    images, seq_col, feat = pixels_tokens.shape
    tokens = images * seq_col
    rows, cols = lax.axis_size("row"), lax.axis_size("col")
    bf16, f32 = jnp.bfloat16, jnp.float32
    width = rows * feat
    wcols, ocols = w_qkv.shape[1], w_out.shape[1]
    heads = cols * w_out.shape[0]
    dma = pltpu.SemaphoreType.DMA
    any_space = pl.BlockSpec(memory_space=pl.ANY)
    vmem = pl.BlockSpec(memory_space=pltpu.VMEM)
    pairs = [dma((8, 2)), dma((8, 2))]
    padded = -(-tokens // 128) * 128
    out = pl.pallas_call(
        block_kernel,
        out_shape=jax.ShapeDtypeStruct((tokens, feat), bf16),
        in_specs=[any_space, vmem, vmem, any_space, any_space],
        out_specs=vmem,
        scratch_shapes=[
            pltpu.VMEM((tokens, width), bf16),
            pltpu.VMEM((tokens, width), bf16),
            pltpu.VMEM((width, wcols), bf16),
            pltpu.VMEM((2, heads // 2, ocols), bf16),
            pltpu.VMEM((tokens, wcols), f32),
            pltpu.VMEM((tokens, wcols), bf16),
            pltpu.VMEM((cols * seq_col, 4 * HDIM), bf16),
            pltpu.VMEM((cols * seq_col, 4 * HDIM), bf16),
            pltpu.VMEM((cols * seq_col // 2, HDIM), bf16),
            pltpu.VMEM((cols * seq_col // 2, HDIM), bf16),
            pltpu.VMEM((tokens, heads // 2), bf16),
            pltpu.VMEM((tokens, heads // 2), bf16),
            pltpu.VMEM((tokens, ocols), f32),
            pltpu.VMEM((rows, 8, padded), f32),
            pltpu.VMEM((2, padded, 128), f32),
            *pairs, *pairs, *pairs, *pairs, *pairs, *pairs, *pairs,
            dma((2, 8)), dma((2, 8)), dma((2, 8)), dma((2, 8)), dma((2, 8)), dma((2, 8)),
            dma((8,)), dma((8,)), dma((4,)),
        ],
        compiler_params=pltpu.CompilerParams(
            collective_id=0, has_side_effects=True, vmem_limit_bytes=61 * 2**20
        ),
        name="attention_block",
    )(pixels_tokens.reshape(tokens, feat), ln_gain.reshape(1, -1), ln_bias.reshape(1, -1), w_qkv, w_out)
    return out.reshape(images, seq_col, feat)


def solution(mesh):
    in_specs = (P(None, "col", "row"), P(), P(), P("col", "row"), P("col", "row"))
    out_specs = P(None, "col", "row")
    return jax.shard_map(local, mesh=mesh, in_specs=in_specs, out_specs=out_specs, check_vma=False)
```

```python
import jax
import jax.numpy as jnp
from jax import lax
from jax.experimental import pallas as pl
from jax.experimental.pallas import tpu as pltpu
from jax.sharding import PartitionSpec as P

HDIM = 128
MESH = pl.DeviceIdType.MESH
HALVES = (0, 1)
OWN, A, BP, BM, CP, CM, D, E = range(8)


def ring(p, step):
    return lax.rem(p + step + 4, 4)


class Gather:
    def __init__(self, p, q, device, block, view, source, sems, last_by_pair, sibling=None):
        self.p, self.q, self.device, self.block = p, q, device, block
        self.view, self.source, self.sems = view, source, sems
        self.last_by_pair, self.sibling = last_by_pair, sibling
        self.sent = []

    def place(self, role):
        p, q, o = self.p, self.q, 1 - self.q
        return {
            OWN: (p, q), A: (p, o), BP: (ring(p, -1), q), BM: (ring(p, 1), q),
            CP: (ring(p, -1), o), CM: (ring(p, 1), o), D: (ring(p, 2), q), E: (ring(p, 2), o),
        }[role]

    def ref(self, role, half):
        return self.view(self.block(*self.place(role)), half)

    def send(self, role, half, there, to):
        send_sem, recv_sem = self.sems[0], self.sems[1]
        src = self.source(half) if role == OWN and self.source is not None else self.ref(role, half)
        copy = pltpu.make_async_remote_copy(
            src_ref=src,
            dst_ref=self.ref(role, half),
            send_sem=send_sem.at[there, half],
            recv_sem=recv_sem.at[there, half],
            device_id=to,
            device_id_type=MESH,
        )
        copy.start()
        self.sent.append(copy)

    def share(self, role, half):
        if self.sibling is None:
            return
        device, view = self.sibling
        send_sem, recv_sem = self.sems[2], self.sems[3]
        src = self.source(half) if role == OWN and self.source is not None else self.ref(role, half)
        copy = pltpu.make_async_remote_copy(
            src_ref=src,
            dst_ref=self.ref(role, half),
            send_sem=send_sem.at[role, half],
            recv_sem=recv_sem.at[role, half],
            device_id=device,
            device_id_type=MESH,
        )
        copy.start()
        self.sent.append(copy)

    def up(self):
        return self.device(ring(self.p, 1), self.q)

    def down(self):
        return self.device(ring(self.p, -1), self.q)

    def across(self):
        return self.device(self.p, 1 - self.q)

    def begin_across(self, half):
        self.send(OWN, half, A, self.across())

    def begin_ring(self, half):
        self.send(OWN, half, BP, self.up())
        self.send(OWN, half, BM, self.down())
        self.share(OWN, half)

    def begin(self, half):
        self.begin_across(half)
        self.begin_ring(half)

    def arrive(self, role, half):
        recv_sem = self.sems[1]
        here = self.ref(role, half)
        pltpu.make_async_copy(here, here, recv_sem.at[role, half]).wait()
        if role == A:
            self.send(A, half, CP, self.up())
            self.send(A, half, CM, self.down())
        elif role == BP and half == 0:
            self.send(BP, half, D, self.up())
        elif role == BM and half == 1:
            self.send(BM, half, D, self.down())
        elif role == D and self.last_by_pair:
            self.send(D, half, E, self.across())
        elif role == CP and half == 0 and not self.last_by_pair:
            self.send(CP, half, E, self.up())
        elif role == CM and half == 1 and not self.last_by_pair:
            self.send(CM, half, E, self.down())
        self.share(role, half)

    def shared(self, role):
        _, view = self.sibling
        for half in HALVES:
            here = view(self.place(role), half)
            pltpu.make_async_copy(here, here, self.sems[3].at[role, half]).wait()

    def finish(self):
        for copy in self.sent:
            copy.wait_send()


def block_kernel(
    x_ref, gain_ref, bias_ref, wq_ref, wo_ref, out_ref,
    xbuf, nbuf, wbuf, wobuf, acc, qkv, item0, item1, hout0, hout1, heads0, heads1, pacc,
    stats, moments,
    xs, xr, ws, wr, wss, wsr, os, orr, oss, osr, hs0, hr0, hs1, hr1,
    as_, ar, ass, asr, bs, br, ms, mr, local_sem,
):
    row, col = lax.axis_index("row"), lax.axis_index("col")
    zh, xx = lax.div(row, 4), lax.rem(row, 4)
    yy, zl, core = lax.div(col, 4), lax.rem(lax.div(col, 2), 2), lax.rem(col, 2)
    plane = lax.div(col, 2)
    tokens, feat = x_ref.shape
    wrows, wcols = wq_ref.shape
    orows, ocols = wo_ref.shape
    seq_col = tokens // 4
    per_head = 3 * HDIM
    items, houts, heads = (item0, item1), (hout0, hout1), (heads0, heads1)
    sibling = (row, plane * 2 + 1 - core)

    def col_device(y, z):
        return (row, y * 4 + z * 2 + core)

    def row_device(x, h):
        return (h * 4 + x, col)

    def plane_peer(d):
        return lax.rem(plane + d, 8)

    def plane_device(p):
        return (row, p * 2 + core)

    def row_peer(d):
        return (lax.rem(row + d, 8), col)

    barrier = pltpu.get_barrier_semaphore()
    for d in range(1, 8):
        pl.semaphore_signal(barrier, inc=1, device_id=plane_device(plane_peer(d)), device_id_type=MESH)
        pl.semaphore_signal(barrier, inc=1, device_id=row_peer(d), device_id_type=MESH)
    pl.semaphore_signal(barrier, inc=1, device_id=sibling, device_id_type=MESH)

    def cols(ref, start, size, rows=None):
        rows = pl.ds(0, tokens) if rows is None else rows
        return ref.at[rows, pl.ds(pl.multiple_of(start, 128), size)]

    half_rows = wrows // 2

    def wq_view(k):
        def view(place, half):
            start = (place[0] * 4 + place[1] * 2 + k) * wrows + half * half_rows
            return wbuf.at[pl.ds(pl.multiple_of(start, 16), half_rows)]

        return view

    def wo_view(k):
        def view(place, half):
            start = (place[0] * 4 + place[1] * 2 + k) * HDIM
            return wobuf.at[half, pl.ds(pl.multiple_of(start, 16), HDIM)]

        return view

    def weight_gather(src, view, sems, last_by_pair):
        size = src.shape[0] // 2
        return Gather(
            yy, zl, col_device, lambda y, z: (y, z), view(core),
            lambda half: src.at[pl.ds(half * size, size)], sems, last_by_pair,
            sibling=(sibling, view(1 - core)),
        )

    half_tokens = tokens // 2

    def row_gather(buf, width, source, sems, last_by_pair):
        return Gather(
            xx, zh, row_device, lambda x, h: h * 4 + x,
            lambda b, half: cols(buf, b * width, width, pl.ds(half * half_tokens, half_tokens)),
            source, sems, last_by_pair,
        )

    gx = row_gather(xbuf, feat, lambda half: x_ref.at[pl.ds(half * half_tokens, half_tokens)], (xs, xr), False)
    gw = weight_gather(wq_ref, wq_view, (ws, wr, wss, wsr), True)
    go = weight_gather(wo_ref, wo_view, (os, orr, oss, osr), False)
    gh = [
        row_gather(heads0, 2 * HDIM, None, (hs0, hr0), True),
        row_gather(heads1, 2 * HDIM, None, (hs1, hr1), True),
    ]

    own = [
        pltpu.make_async_copy(x_ref, cols(xbuf, row * feat, feat), local_sem.at[0]),
        pltpu.make_async_copy(wq_ref, wbuf.at[pl.ds(pl.multiple_of(col * wrows, 16), wrows)], local_sem.at[1]),
        pltpu.make_async_copy(wo_ref.at[pl.ds(0, HDIM)], wo_view(core)((yy, zl), 0), local_sem.at[2]),
        pltpu.make_async_copy(wo_ref.at[pl.ds(HDIM, HDIM)], wo_view(core)((yy, zl), 1), local_sem.at[3]),
    ]
    for copy in own:
        copy.start()
    pl.semaphore_wait(barrier, 15)

    for half in HALVES:
        gx.begin(half)
        gw.begin_ring(half)
    for copy in own:
        copy.wait()

    chunk = 96
    means, rates = moments.at[0], moments.at[1]
    padded = moments.shape[1]
    means[...] = jnp.zeros_like(means)

    @pl.loop(0, tokens // chunk)
    def _(i):
        rows = pl.ds(pl.multiple_of(i * chunk, chunk), chunk)
        floats = xbuf[rows, pl.ds(pl.multiple_of(row * feat, 128), feat)].astype(jnp.float32)
        center = jnp.sum(floats, axis=-1, keepdims=True) * (1.0 / feat)
        moved = floats - center
        square = jnp.sum(moved * moved, axis=-1, keepdims=True)
        lane = lax.broadcasted_iota(jnp.int32, (chunk, 128), 1)
        means[rows, :] = jnp.where(lane == 0, center, jnp.where(lane == 1, square, 0.0))

    stats[row] = means[...].T[:8]
    told = []
    for d in range(1, 8):
        copy = pltpu.make_async_remote_copy(
            src_ref=stats.at[row], dst_ref=stats.at[row], send_sem=ms.at[d], recv_sem=mr.at[d],
            device_id=row_peer(d), device_id_type=MESH,
        )
        copy.start()
        told.append(copy)
    for item in items:
        item[:, 3 * HDIM :] = jnp.ones((item.shape[0], HDIM), jnp.bfloat16)

    gx.arrive(A, 0)
    gw.begin_across(0)
    gx.arrive(BP, 0)
    gx.arrive(BM, 0)
    for d in range(1, 8):
        here = stats.at[lax.rem(row - d + 8, 8)]
        pltpu.make_async_copy(here, here, mr.at[d]).wait()
    centers = stats[:, 0, :]
    mean = jnp.sum(centers, axis=0, keepdims=True) * (1.0 / 8)
    off = centers - mean
    square = jnp.sum(stats[:, 1, :], axis=0, keepdims=True) + jnp.sum(off * off, axis=0, keepdims=True) * feat
    rate = lax.rsqrt(square * (1.0 / (8 * feat)) + 1e-06)
    means[...] = jnp.broadcast_to(mean, (128, padded)).T
    rates[...] = jnp.broadcast_to(rate, (128, padded)).T

    def normalise(role):
        start = gx.block(*gx.place(role)) * feat

        @pl.loop(0, tokens // chunk)
        def _(i):
            rows = pl.ds(pl.multiple_of(i * chunk, chunk), chunk)
            mean, rate = means[rows, :], rates[rows, :]
            for step in range(feat // 128):
                columns = pl.ds(pl.multiple_of(start + step * 128, 128), 128)
                floats = xbuf[rows, columns].astype(jnp.float32)
                nbuf[rows, columns] = (
                    (floats - mean) * rate * gain_ref[:, columns] + bias_ref[:, columns]
                ).astype(jnp.bfloat16)

    normalise(OWN)
    gw.arrive(BP, 0)
    gw.arrive(BM, 0)
    gx.arrive(A, 1)
    gw.begin_across(1)
    gx.arrive(BP, 1)
    gx.arrive(BM, 1)
    normalise(A)
    normalise(BP)
    normalise(BM)
    gw.arrive(BP, 1)
    gw.arrive(BM, 1)
    gw.arrive(A, 0)
    gx.arrive(CP, 0)
    gx.arrive(CM, 0)
    gw.arrive(D, 0)
    gw.arrive(D, 1)
    gw.arrive(A, 1)
    gx.arrive(CP, 1)
    gx.arrive(CM, 1)
    normalise(CP)
    normalise(CM)
    gx.arrive(D, 0)
    gx.arrive(D, 1)
    normalise(D)
    gx.arrive(E, 0)
    gx.arrive(E, 1)
    normalise(E)

    unit = 2 * wrows

    def product(place, columns):
        at = pl.multiple_of((place[0] * 2 + place[1]) * unit, 128)
        return jnp.dot(
            nbuf[:, pl.ds(at, unit)], wbuf[pl.ds(at, unit), columns], preferred_element_type=jnp.float32
        )

    def multiply(role, first=False):
        gw.shared(role)
        place = gw.place(role)

        @pl.loop(0, wcols // 256)
        def _(j):
            columns = pl.ds(pl.multiple_of(j * 256, 256), 256)
            if first:
                acc[:, columns] = product(place, columns)
            else:
                acc[:, columns] += product(place, columns)

    multiply(OWN, first=True)
    multiply(BP)
    multiply(BM)
    multiply(A)
    gw.arrive(CP, 0)
    gw.arrive(CM, 0)
    multiply(D)
    gw.arrive(E, 0)
    gw.arrive(CP, 1)
    gw.arrive(CM, 1)
    gw.arrive(E, 1)
    for half in HALVES:
        go.begin_across(half)
    for role in (CP, CM, E):
        gw.shared(role)

    def rows_of(p):
        return pl.ds(pl.multiple_of(p * seq_col, 16), seq_col)

    def to_attend(wave, d):
        p = plane_peer(d)
        start = pl.multiple_of((lax.rem(p, 2) * 2 + wave) * per_head, 128)
        src = qkv.at[rows_of(lax.div(p, 2)), pl.ds(start, per_head)]
        dst = items[wave].at[rows_of(plane), pl.ds(0, per_head)]
        return src, dst, plane_device(p)

    attending = []

    across_first = (1, 3, 5, 7, 2, 4, 6)

    def complete(wave, z):
        columns = pl.ds(pl.multiple_of((z * 2 + wave) * per_head, 128), per_head)
        total = acc[:, columns]
        for role in (CP, CM, E):
            total += product(gw.place(role), columns)
        qkv[:, columns] = total.astype(jnp.bfloat16)

    def attend_send(wave, distances):
        for d in distances:
            src, dst, device = to_attend(wave, d)
            copy = pltpu.make_async_remote_copy(
                src_ref=src, dst_ref=dst, send_sem=as_.at[wave, d], recv_sem=ar.at[wave, d],
                device_id=device, device_id_type=MESH,
            )
            copy.start()
            attending.append(copy)

    def attend_keep(wave):
        src, dst, _ = to_attend(wave, 0)
        mine = pltpu.make_async_copy(src, dst, local_sem.at[wave])
        mine.start()
        return mine

    both = pl.ds(HDIM, 2 * HDIM)

    def keys_share(wave, d):
        p = lax.rem(plane - d + 8, 8)
        copy = pltpu.make_async_remote_copy(
            src_ref=items[wave].at[rows_of(p), both], dst_ref=items[wave].at[rows_of(p + 8), both],
            send_sem=ass.at[wave, d], recv_sem=asr.at[wave, d],
            device_id=sibling, device_id_type=MESH,
        )
        copy.start()
        attending.append(copy)

    def attend_receive(wave, mine):
        mine.wait()
        keys_share(wave, 0)
        for d in across_first:
            here = items[wave].at[rows_of(lax.rem(plane - d + 8, 8)), pl.ds(0, per_head)]
            pltpu.make_async_copy(here, here, ar.at[wave, d]).wait()
            keys_share(wave, d)
        for d in range(8):
            here = items[wave].at[rows_of(lax.rem(plane - d + 8, 8) + 8), both]
            pltpu.make_async_copy(here, here, asr.at[wave, d]).wait()

    def back_view(wave, p):
        start = pl.multiple_of(row * 2 * HDIM + lax.rem(p, 2) * HDIM, 128)
        return heads[wave].at[rows_of(lax.div(p, 2)), pl.ds(start, HDIM)]

    def back(wave, d):
        p = plane_peer(d)
        return pltpu.make_async_remote_copy(
            src_ref=houts[wave].at[rows_of(p)], dst_ref=back_view(wave, plane),
            send_sem=bs.at[wave, d], recv_sem=br.at[wave, d],
            device_id=plane_device(p), device_id_type=MESH,
        )

    power = HDIM ** (-0.5) * 1.4426950408889634

    def attend(wave, d):
        item, rows = items[wave], rows_of(plane_peer(d))
        scores = lax.dot_general(
            item[rows, :HDIM], item[:, HDIM : 2 * HDIM], (((1,), (1,)), ((), ())),
            preferred_element_type=jnp.float32,
        )
        peak = jnp.max(scores, axis=-1, keepdims=True)
        expo = jnp.exp2((scores - peak) * power).astype(jnp.bfloat16)
        mixed = jnp.dot(expo, item[:, 2 * HDIM :], preferred_element_type=jnp.float32)
        houts[wave][rows, :] = (mixed[:, :HDIM] / mixed[:, HDIM:]).astype(jnp.bfloat16)

    def attention(wave, group):
        order = range(4 * group + 1, 4 * group + 5)
        for d in order:
            attend(wave, d)
        for d in order:
            if d < 8:
                back(wave, d).start()
            else:
                mine = pltpu.make_async_copy(houts[wave].at[rows_of(plane)], back_view(wave, plane), local_sem.at[2])
                mine.start()
                mine.wait()

    def back_receive(wave):
        for d in range(1, 8):
            here = back_view(wave, lax.rem(plane - d + 8, 8))
            pltpu.make_async_copy(here, here, br.at[wave, d]).wait()
        for half in HALVES:
            gh[wave].begin(half)

    def near(gather, half):
        for role in (BP, BM, A):
            gather.arrive(role, half)

    complete(0, 1 - zl)
    attend_send(0, (1, 3, 5, 7))
    complete(0, zl)
    attend_send(0, (2, 4, 6))
    mine0 = attend_keep(0)
    complete(1, 1 - zl)
    complete(1, zl)
    attend_receive(0, mine0)
    attend_send(1, across_first)
    mine1 = attend_keep(1)
    attention(0, 0)
    attention(0, 1)
    for half in HALVES:
        go.begin_ring(half)
    back_receive(0)
    attend_receive(1, mine1)
    attention(1, 0)
    near(gh[0], 0)
    near(go, 0)
    near(go, 1)
    attention(1, 1)
    near(gh[0], 1)
    gh[0].arrive(D, 0)
    gh[0].arrive(D, 1)
    back_receive(1)

    for half in HALVES:
        go.arrive(CP, half)
        go.arrive(CM, half)
    for half in HALVES:
        go.arrive(D, half)
    near(gh[1], 0)
    near(gh[1], 1)
    for half in HALVES:
        go.arrive(E, half)
    gh[1].arrive(D, 0)
    gh[1].arrive(D, 1)
    for role in range(8):
        go.shared(role)

    def part(wave, role):
        at = pl.multiple_of(gh[wave].block(*gh[wave].place(role)) * 2 * HDIM, 128)
        return jnp.dot(
            heads[wave][:, pl.ds(at, 2 * HDIM)], wobuf[wave, pl.ds(at, 2 * HDIM), :],
            preferred_element_type=jnp.float32,
        )

    def project(*terms):
        total = pacc[...]
        for wave, role in terms:
            total += part(wave, role)
        pacc[...] = total

    pacc[...] = xbuf[:, pl.ds(pl.multiple_of(row * feat, 128), feat)].astype(jnp.float32)
    project((0, OWN), (0, BP), (0, BM), (0, A), (0, D))
    for half in HALVES:
        for role in (CP, CM, E):
            gh[0].arrive(role, half)
    project((0, CP), (0, CM), (0, E), (1, OWN), (1, BP), (1, BM), (1, A), (1, D))
    for half in HALVES:
        for role in (CP, CM, E):
            gh[1].arrive(role, half)
    out_ref[...] = (pacc[...] + part(1, CP) + part(1, CM) + part(1, E)).astype(jnp.bfloat16)

    for gather in (gx, gw, go, *gh):
        gather.finish()
    for copy in told + attending:
        copy.wait_send()
    for wave in range(2):
        for d in range(1, 8):
            back(wave, d).wait_send()


def local(pixels_tokens, ln_gain, ln_bias, w_qkv, w_out):
    images, seq_col, feat = pixels_tokens.shape
    tokens = images * seq_col
    rows, cols = lax.axis_size("row"), lax.axis_size("col")
    bf16, f32 = jnp.bfloat16, jnp.float32
    width = rows * feat
    wcols, ocols = w_qkv.shape[1], w_out.shape[1]
    heads = cols * w_out.shape[0]
    dma = pltpu.SemaphoreType.DMA
    any_space = pl.BlockSpec(memory_space=pl.ANY)
    vmem = pl.BlockSpec(memory_space=pltpu.VMEM)
    pairs = [dma((8, 2)), dma((8, 2))]
    padded = -(-tokens // 128) * 128
    out = pl.pallas_call(
        block_kernel,
        out_shape=jax.ShapeDtypeStruct((tokens, feat), bf16),
        in_specs=[any_space, vmem, vmem, any_space, any_space],
        out_specs=vmem,
        scratch_shapes=[
            pltpu.VMEM((tokens, width), bf16),
            pltpu.VMEM((tokens, width), bf16),
            pltpu.VMEM((width, wcols), bf16),
            pltpu.VMEM((2, heads // 2, ocols), bf16),
            pltpu.VMEM((tokens, wcols), f32),
            pltpu.VMEM((tokens, wcols), bf16),
            pltpu.VMEM((cols * seq_col, 4 * HDIM), bf16),
            pltpu.VMEM((cols * seq_col, 4 * HDIM), bf16),
            pltpu.VMEM((cols * seq_col // 2, HDIM), bf16),
            pltpu.VMEM((cols * seq_col // 2, HDIM), bf16),
            pltpu.VMEM((tokens, heads // 2), bf16),
            pltpu.VMEM((tokens, heads // 2), bf16),
            pltpu.VMEM((tokens, ocols), f32),
            pltpu.VMEM((rows, 8, padded), f32),
            pltpu.VMEM((2, padded, 128), f32),
            *pairs, *pairs, *pairs, *pairs, *pairs, *pairs, *pairs,
            dma((2, 8)), dma((2, 8)), dma((2, 8)), dma((2, 8)), dma((2, 8)), dma((2, 8)),
            dma((8,)), dma((8,)), dma((4,)),
        ],
        compiler_params=pltpu.CompilerParams(
            collective_id=0, has_side_effects=True, vmem_limit_bytes=61 * 2**20
        ),
        name="attention_block",
    )(pixels_tokens.reshape(tokens, feat), ln_gain.reshape(1, -1), ln_bias.reshape(1, -1), w_qkv, w_out)
    return out.reshape(images, seq_col, feat)


def solution(mesh):
    in_specs = (P(None, "col", "row"), P(), P(), P("col", "row"), P("col", "row"))
    out_specs = P(None, "col", "row")
    return jax.shard_map(local, mesh=mesh, in_specs=in_specs, out_specs=out_specs, check_vma=False)
```
